256 devices in a mesh: ctx: 32 (over z_hi, x, y), tensor: 8 (over z_lo, core).
Axes of the slice: x: 4, y: 4, z: 8 (z_hi: 2, z_lo: 4; z = z_hi * 4 + z_lo), core: 2. Of those that a mesh axis runs over, the one named last changes fastest.
Arguments:
- query_rows: bfloat16 [4096, 8192], P('ctx', 'tensor'), may hold values from -6 to 6
- key_rows: bfloat16 [4096, 8192], P('ctx', 'tensor'), may hold values from -6 to 6
- value_rows: bfloat16 [4096, 8192], P('ctx', 'tensor'), may hold values from -6 to 6
- grad_rows: bfloat16 [4096, 8192], P('ctx', 'tensor'), may hold values from -6 to 6
- residues: float32 [512, 16], replicated, may hold values from -0.25 to 0.25
- decay_rates: float32 [512, 16], replicated, may hold values from 0.00012207031 to 0.05
Outputs:
- operator_out: bfloat16 [4096, 8192], P('ctx', 'tensor')
- grad_query: bfloat16 [4096, 8192], P('ctx', 'tensor')
- grad_key: bfloat16 [4096, 8192], P('ctx', 'tensor')
- grad_value: bfloat16 [4096, 8192], P('ctx', 'tensor')
- grad_residues: float32 [512, 16], replicated
- grad_rates: float32 [512, 16], replicated
The draws below stay inside these ranges and needn't reach their ends.
All inputs are finite; a program needn't handle non-finite values.
Results may differ from the reference program's by a relative error of at most 0.013.
Values may be sent and summed in bfloat16 or wider, within the bound.
A program may use at most 192 MiB of HBM per device.

```python
import math
import jax
import jax.numpy as jnp
from jax import lax

W = 8192
FILTERS = 512
ORDER = 16
TOKENS = 4096


def block_levels(own_key, extent, cuts, low, top_value):
    def one(dim, parts):
        heights = jax.random.uniform(jax.random.fold_in(jax.random.fold_in(own_key, 6), dim), (parts,), jnp.float32, low / len(cuts), top_value / len(cuts))
        return jnp.repeat(jnp.exp(heights), extent[dim] // parts).reshape((-1,) + (1,) * (len(extent) - dim - 1))

    factor_of = one(*cuts[0])
    for cut in cuts[1:]:
        factor_of = factor_of * one(*cut)
    return factor_of


def normal_values(key, extent, spread, reach, cuts=(), kind=jnp.bfloat16):
    values = spread * jax.random.normal(key, extent, jnp.float32)
    if cuts:
        values = values * block_levels(key, extent, cuts, -0.22, 0.18)
    return jnp.clip(values, -reach, reach).astype(kind)


def setup_inputs(seed: int = 0) -> dict:
    key_list = jax.random.split(jax.random.key(seed), 7)
    return {
        "query_rows": normal_values(key_list[0], (TOKENS, W), 1.0, 6.0, ((0, 32), (1, 8))),
        "key_rows": normal_values(key_list[1], (TOKENS, W), 1.0, 6.0, ((0, 32), (1, 8))),
        "value_rows": normal_values(key_list[2], (TOKENS, W), 1.0, 6.0, ((0, 32), (1, 8))),
        "grad_rows": normal_values(key_list[3], (TOKENS, W), 1.0, 6.0, ((0, 32), (1, 8))),
        "residues": normal_values(key_list[4], (FILTERS, ORDER), 0.05, 0.25, (), jnp.float32),
        "decay_rates": jnp.clip(jnp.exp(jax.random.uniform(key_list[5], (FILTERS, ORDER), jnp.float32, math.log(0.00012207031), math.log(0.05))), 0.00012207031, 0.05),
    }


def rounded(values):
    return lax.optimization_barrier(values.astype(jnp.bfloat16)).astype(jnp.float32)

def reference(query_rows, key_rows, value_rows, grad_rows, residues, decay_rates):
    seq_len = TOKENS
    group_size = W // FILTERS
    per_piece = 4
    piece_count = FILTERS // per_piece
    chan_piece = per_piece * group_size
    gated = rounded(query_rows.astype(jnp.float32) * key_rows.astype(jnp.float32))
    gated_grad = rounded(grad_rows.astype(jnp.float32) * value_rows.astype(jnp.float32))
    gated_parts = gated.reshape(seq_len, piece_count, chan_piece).transpose(1, 0, 2)
    grad_parts = gated_grad.reshape(seq_len, piece_count, chan_piece).transpose(1, 0, 2)

    def convolve(res_f, rate_f, inputs):
        res_c = jnp.repeat(res_f, group_size, axis=0)
        rate_c = jnp.repeat(rate_f, group_size, axis=0)
        lags = jnp.arange(seq_len).astype(res_c.dtype)
        kernel = lax.optimization_barrier(jnp.sum(res_c[:, :, None] * jnp.exp(-rate_c[:, :, None] * lags), axis=1))
        spectrum = jnp.fft.rfft(kernel, n=2 * seq_len, axis=1) * jnp.fft.rfft(inputs.T, n=2 * seq_len, axis=1)
        return jnp.fft.irfft(spectrum, n=2 * seq_len, axis=1)[:, :seq_len].T

    def one_piece(packed):
        res_f, rate_f, inputs, cotangent = packed
        conv_out, pullback = jax.vjp(convolve, res_f, rate_f, inputs)
        d_res, d_rate, d_inputs = pullback(cotangent)
        return (conv_out, d_inputs, d_res, d_rate)
    conv_all, back_all, d_res, d_rate = lax.map(one_piece, (residues.reshape(piece_count, per_piece, ORDER), decay_rates.reshape(piece_count, per_piece, ORDER), gated_parts, grad_parts))
    conv_rows = rounded(conv_all.transpose(1, 0, 2).reshape(seq_len, W))
    back_rows = rounded(back_all.transpose(1, 0, 2).reshape(seq_len, W))
    operator_out = (value_rows.astype(jnp.float32) * conv_rows).astype(jnp.bfloat16)
    grad_value = (grad_rows.astype(jnp.float32) * conv_rows).astype(jnp.bfloat16)
    grad_query = (back_rows * key_rows.astype(jnp.float32)).astype(jnp.bfloat16)
    grad_key = (back_rows * query_rows.astype(jnp.float32)).astype(jnp.bfloat16)
    return (operator_out, grad_query, grad_key, grad_value, d_res.reshape(FILTERS, ORDER), d_rate.reshape(FILTERS, ORDER))
```

```python
import functools

import jax
import jax.numpy as jnp
from jax import lax
from jax.experimental import pallas as pl
from jax.experimental.pallas import tpu as pltpu
from jax.sharding import PartitionSpec as P

MESH = pl.DeviceIdType.MESH
F32 = jnp.float32
BF16 = jnp.bfloat16
EXACT = lax.Precision.HIGHEST

TOK = 128
CHUNKS = 8
PER = 8
GROUP = 16
MODES = 16
PLANE = 16


def iota(shape, dim):
    return lax.broadcasted_iota(jnp.int32, shape, dim)


def dot(a, b, precision=None):
    return lax.dot_general(
        a, b, (((1,), (0,)), ((), ())), precision=precision, preferred_element_type=F32
    )


def dot_nt(a, b):
    return lax.dot_general(a, b, (((1,), (1,)), ((), ())), preferred_element_type=F32)


def kernel(
    q_hbm, k_hbm, v_hbm, g_hbm, res_hbm, rate_hbm,
    op_ref, gq_ref, gk_ref, gv_ref, gres_ref, grate_ref,
    q_v, k_v, v_v, g_v, par, wst, hrev, acoef, rhs, local, lagrev,
    send1, recv1, gsend, grecv, zsend, zrecv, fstate, bstate, send2, recv2, tsend, trecv,
    in_sem, par_sem, send_sem, recv1_sem, recvg_sem, recvz_sem, recv2_sem, recvt_sem,
):
    ctx = lax.axis_index("ctx")
    tau = lax.axis_index("tensor")
    plane = ctx // PLANE
    me = ctx % PLANE
    base = plane * PLANE

    lanes = pl.ds(pl.multiple_of((tau // 2) * 128, 128), 128)
    par_copies = [
        pltpu.make_async_copy(res_hbm.at[:, lanes], par.at[0], par_sem.at[0]),
        pltpu.make_async_copy(rate_hbm.at[:, lanes], par.at[1], par_sem.at[1]),
    ]
    in_copies = [
        pltpu.make_async_copy(src, dst, in_sem.at[i])
        for i, (src, dst) in enumerate(((q_hbm, q_v), (k_hbm, k_v), (g_hbm, g_v), (v_hbm, v_v)))
    ]
    for copy in par_copies + in_copies:
        copy.start()

    barrier = pltpu.get_barrier_semaphore()

    @pl.loop(1, PLANE)
    def _(i):
        pl.semaphore_signal(
            barrier, inc=1, device_id={"ctx": base + (me + i) % PLANE}, device_id_type=MESH
        )

    pl.semaphore_signal(
        barrier, inc=1, device_id={"ctx": (1 - plane) * PLANE + me}, device_id_type=MESH
    )

    @pl.loop(1, 8)
    def _(i):
        pl.semaphore_signal(
            barrier, inc=1, device_id={"tensor": (tau + i) % 8}, device_id_type=MESH
        )

    for copy in par_copies:
        copy.wait()

    lane16 = iota((MODES, 128), 1)
    odd = (tau % 2) == 1

    def own_half(x):
        rolled = pltpu.roll(x, 64, 1)
        first = jnp.where(odd, rolled, x)
        return jnp.where(lane16 < 64, first, jnp.where(odd, x, rolled))

    res_t = own_half(par[0])
    rate_t = own_half(par[1])

    behind = (127 - lane16).astype(F32)
    ahead = (lane16 + 1).astype(F32)

    @pl.loop(0, CHUNKS)
    def _(k):
        shift = (128 - PER * k) % 128
        res_k = pltpu.roll(res_t, shift, 1)
        rate_k = pltpu.roll(rate_t, shift, 1)
        powers = []
        for i in range(PER):
            rate = rate_k[:, i : i + 1]
            res = res_k[:, i : i + 1]
            decay = jnp.exp(-rate * behind)
            wst[k * PER + i, 0:16, :] = decay.astype(BF16)
            wst[k * PER + i, 16:32, :] = (decay * behind).astype(BF16)
            hrev[k, i : i + 1, :] = jnp.sum(res * decay, axis=0, keepdims=True)
            powers.append(res * jnp.exp(-rate * ahead))
        acoef[k] = jnp.concatenate(powers, axis=0).T.astype(BF16)

    for copy in in_copies:
        copy.wait()

    turn = (iota((TOK, TOK), 0) + iota((TOK, TOK), 1) == TOK - 1).astype(BF16)
    group_of = (iota((1, 256), 1) % 128) // GROUP

    @pl.loop(0, CHUNKS)
    def _(k):
        cols = pl.ds(pl.multiple_of(k * 128, 128), 128)
        u = (q_v[:, cols].astype(F32) * k_v[:, cols].astype(F32)).astype(BF16)
        dz = (g_v[:, cols].astype(F32) * v_v[:, cols].astype(F32)).astype(BF16)
        rhs[k, :, 0:128] = u
        rhs[k, :, 128:256] = dot(turn, dz).astype(BF16)
        weights = wst[pl.ds(k * PER, PER)].reshape(PER * 32, TOK)
        ends = dot(weights, rhs[k])
        total = jnp.zeros((32, 256), F32)
        for i in range(PER):
            total = jnp.where(group_of == i, ends[32 * i : 32 * i + 32], total)
        for h in range(2):
            rows = slice(8 * h, 8 * h + 8)
            rows2 = slice(16 + 8 * h, 24 + 8 * h)
            send1[2 * k + h] = jnp.concatenate(
                [
                    total[rows, 0:128],
                    total[rows, 128:256],
                    total[rows2, 0:128],
                    total[rows2, 128:256],
                ],
                axis=0,
            ).astype(BF16)

    pl.semaphore_wait(barrier, PLANE - 1 + 1 + 7)

    @pl.loop(1, PLANE)
    def _(i):
        peer = (me + i) % PLANE
        pltpu.make_async_remote_copy(
            src_ref=send1.at[peer],
            dst_ref=recv1.at[me],
            send_sem=send_sem.at[0],
            recv_sem=recv1_sem,
            device_id={"ctx": base + peer},
            device_id_type=MESH,
        ).start()

    recv1[me] = send1[me]

    row = iota((TOK, TOK), 0)
    lane = iota((TOK, TOK), 1)

    @pl.loop(0, CHUNKS)
    def _(k):
        u = rhs[k, :, 0:128]
        dz = rhs[k, :, 128:256]
        for i in range(PER):
            mine = jnp.where(group_of[:, 0:128] == i, dz, jnp.zeros_like(dz))
            pairs = dot_nt(mine, u)
            diag = pltpu.roll(pairs, 0, 1, stride=1, stride_axis=0)
            lagrev[k, i : i + 1, :] = jnp.sum(
                jnp.where(lane >= row, diag, 0.0), axis=0, keepdims=True
            )

    lag_all = lagrev[...].reshape(64, 128).astype(BF16)
    lag_all = jnp.concatenate([lag_all, lag_all], axis=0)
    lane_filter = iota((32, 128), 1)
    kind_filter = jnp.where(iota((32, 128), 0) < 16, lane_filter, lane_filter - 64)

    def add_filter(k, total):
        part = dot_nt(wst[pl.ds(k * PER, PER)].reshape(PER * 32, TOK), lag_all)
        for i in range(PER):
            total = jnp.where(kind_filter == k * PER + i, part[32 * i : 32 * i + 32], total)
        return total

    local_sums = lax.fori_loop(0, CHUNKS, add_filter, jnp.zeros((32, 128), F32))
    local_sums = local_sums[0:16] + local_sums[16:32]
    gsend[0] = local_sums[0:8]
    gsend[1] = local_sums[8:16]

    @pl.loop(1, PLANE)
    def _(i):
        peer = (me + i) % PLANE
        pltpu.make_async_remote_copy(
            src_ref=gsend.at[peer % 2],
            dst_ref=grecv.at[me],
            send_sem=send_sem.at[1],
            recv_sem=recvg_sem,
            device_id={"ctx": base + peer},
            device_id_type=MESH,
        ).start()

    grecv[me] = gsend[me % 2]

    own_chunk = me // 2
    own_half_id = me % 2
    spread = (iota((128, 128), 0) == PER * own_chunk + iota((128, 128), 1) // GROUP).astype(F32)
    rate_spread = dot(rate_t, spread, EXACT)
    rate_own = jnp.where(own_half_id == 0, rate_spread[0:8], rate_spread[8:16])
    res_own = jnp.where(own_half_id == 0, res_t[0:8], res_t[8:16])
    step = jnp.exp(-rate_own * float(TOK))
    single = jnp.exp(-rate_own)
    collect_lane = iota((128, 128), 1)
    collect_from = PER * own_chunk + iota((128, 128), 0) // GROUP
    collect_one = (collect_lane == collect_from).astype(F32)
    collect_two = (collect_lane == collect_from + 64).astype(F32)

    pltpu.make_async_copy(
        recv1.at[pl.ds(0, PLANE - 1)], recv1.at[pl.ds(0, PLANE - 1)], recv1_sem
    ).wait()

    zero = jnp.zeros((8, 128), F32)
    one, two, sum_one, sum_two = zero, zero, zero, zero
    for m in range(PLANE):
        block = recv1[m].astype(F32)
        end_one, start_one = block[0:8], block[8:16]
        end_two, start_two = block[16:24], block[24:32]
        fstate[m] = one
        sum_one = sum_one + one * start_one
        sum_two = sum_two + two * start_one + one * (start_two + start_one)
        two = step * (two + float(TOK) * one) + end_two
        one = step * one + end_one
    ahead_one, ahead_two = one, two
    one, two = zero, zero
    for m in reversed(range(PLANE)):
        block = recv1[m].astype(F32)
        start_one, start_two = block[8:16], block[24:32]
        bstate[m] = one
        two = step * (two + float(TOK) * one) + start_two
        one = step * one + start_one
    low = plane == 0
    mine_one = jnp.where(low, ahead_one, one)
    mine_two = jnp.where(low, ahead_two, two)

    pltpu.make_async_copy(
        grecv.at[pl.ds(0, PLANE - 1)], grecv.at[pl.ds(0, PLANE - 1)], recvg_sem
    ).wait()
    grads = jnp.sum(grecv[...], axis=0)
    grads = jnp.where((iota((8, 128), 1) % 64) // PER == own_chunk, grads, 0.0)
    grads = grads + dot(single * sum_one, collect_one, EXACT)
    grads = grads + dot(single * sum_two, collect_two, EXACT)
    zsend[0:8] = mine_one
    zsend[8:16] = mine_two
    zsend[16:24] = grads
    z_copy = pltpu.make_async_remote_copy(
        src_ref=zsend,
        dst_ref=zrecv,
        send_sem=send_sem.at[2],
        recv_sem=recvz_sem,
        device_id={"ctx": (1 - plane) * PLANE + me},
        device_id_type=MESH,
    )
    z_copy.start()

    @pl.loop(0, CHUNKS)
    def _(k):
        both = rhs[k]
        total = jnp.zeros((TOK, 256), F32)
        for i in range(PER):
            taps = pltpu.roll(
                jnp.broadcast_to(hrev[k, i : i + 1, :], (TOK, TOK)), 1, 1, stride=1, stride_axis=0
            )
            taps = jnp.where(lane <= row, taps, 0.0).astype(BF16)
            total = jnp.where(group_of == i, dot(taps, both), total)
        local[k] = total

    z_copy.wait_recv()
    other_one, other_two = zrecv[0:8], zrecv[8:16]
    cross_one = single * mine_one * other_one
    cross_two = single * (
        mine_two * other_one + mine_one * other_two + mine_one * other_one
    )
    grads = grads + zrecv[16:24]
    grads = grads + dot(cross_one, collect_one, EXACT) + dot(cross_two, collect_two, EXACT)
    grads = jnp.where(iota((8, 128), 1) < 64, grads, -res_own * grads)
    grads_high = grads.astype(BF16).astype(F32)
    grads_low = grads - grads_high
    into_f = jnp.where(low, 0.0, other_one)
    into_b = jnp.where(low, other_one, 0.0)
    for m in range(PLANE):
        fstate[m] = fstate[m] + into_f
        into_f = step * into_f
    for m in reversed(range(PLANE)):
        send2[m] = jnp.concatenate(
            [fstate[m], bstate[m] + into_b, grads_high, grads_low], axis=0
        ).astype(BF16)
        into_b = step * into_b

    @pl.loop(1, PLANE)
    def _(i):
        peer = (me + i) % PLANE
        pltpu.make_async_remote_copy(
            src_ref=send2.at[peer],
            dst_ref=recv2.at[me],
            send_sem=send_sem.at[3],
            recv_sem=recv2_sem,
            device_id={"ctx": base + peer},
            device_id_type=MESH,
        ).start()

    recv2[me] = send2[me]
    pltpu.make_async_copy(
        recv2.at[pl.ds(0, PLANE - 1)], recv2.at[pl.ds(0, PLANE - 1)], recv2_sem
    ).wait()

    halves = []
    for h in range(2):
        total = jnp.zeros((8, 128), F32)
        for k in range(CHUNKS):
            block = recv2[2 * k + h].astype(F32)
            total = total + (block[16:24] + block[24:32])
        halves.append(total)
    tsend[...] = jnp.concatenate(halves, axis=0)

    @pl.loop(1, 8)
    def _(i):
        pltpu.make_async_remote_copy(
            src_ref=tsend,
            dst_ref=trecv.at[tau],
            send_sem=send_sem.at[4],
            recv_sem=recvt_sem,
            device_id={"tensor": (tau + i) % 8},
            device_id_type=MESH,
        ).start()

    trecv[tau] = tsend[...]

    block_diagonal = (iota((PER, MODES, 256), 2) % 128) // GROUP == iota((PER, MODES, 256), 0)

    @pl.loop(0, CHUNKS)
    def _(k):
        cols = pl.ds(pl.multiple_of(k * 128, 128), 128)
        first = recv2[2 * k].astype(F32)
        second = recv2[2 * k + 1].astype(F32)
        states = jnp.concatenate(
            [
                jnp.concatenate([first[0:8], second[0:8]], axis=0),
                jnp.concatenate([first[8:16], second[8:16]], axis=0),
            ],
            axis=1,
        )
        states = jnp.where(block_diagonal, states[None], 0.0).reshape(PER * MODES, 256)
        total = local[k] + dot(acoef[k], states.astype(BF16))
        conv = total[:, 0:128].astype(BF16).astype(F32)
        back = dot(turn, total[:, 128:256].astype(BF16))
        op_ref[:, cols] = (v_v[:, cols].astype(F32) * conv).astype(BF16)
        gv_ref[:, cols] = (g_v[:, cols].astype(F32) * conv).astype(BF16)
        gq_ref[:, cols] = (k_v[:, cols].astype(F32) * back).astype(BF16)
        gk_ref[:, cols] = (q_v[:, cols].astype(F32) * back).astype(BF16)

    pltpu.make_async_copy(trecv.at[pl.ds(0, 7)], trecv.at[pl.ds(0, 7)], recvt_sem).wait()
    for j in range(4):
        even, uneven = trecv[2 * j], trecv[2 * j + 1]
        gres_ref[:, 128 * j : 128 * j + 128] = jnp.where(
            lane16 < 64, even, pltpu.roll(uneven, 64, 1)
        )
        grate_ref[:, 128 * j : 128 * j + 128] = jnp.where(
            lane16 < 64, pltpu.roll(even, 64, 1), uneven
        )

    def sent(ref, count, sem):
        pltpu.make_async_copy(ref.at[pl.ds(0, count)], ref.at[pl.ds(0, count)], sem).wait()

    sent(send1, PLANE - 1, send_sem.at[0])
    sent(grecv, PLANE - 1, send_sem.at[1])
    z_copy.wait_send()
    sent(send2, PLANE - 1, send_sem.at[3])
    sent(trecv, 7, send_sem.at[4])


def per_device(query_rows, key_rows, value_rows, grad_rows, residues, decay_rates):
    rows, width = query_rows.shape
    any_spec = pl.BlockSpec(memory_space=pl.ANY)
    vmem_spec = pl.BlockSpec(memory_space=pltpu.VMEM)
    wide = jax.ShapeDtypeStruct((rows, width), BF16)
    small = jax.ShapeDtypeStruct((MODES, 512), F32)
    dma = pltpu.SemaphoreType.DMA
    outs = pl.pallas_call(
        kernel,
        out_shape=(wide, wide, wide, wide, small, small),
        in_specs=[any_spec] * 6,
        out_specs=[vmem_spec] * 6,
        scratch_shapes=[
            pltpu.VMEM((rows, width), BF16),
            pltpu.VMEM((rows, width), BF16),
            pltpu.VMEM((rows, width), BF16),
            pltpu.VMEM((rows, width), BF16),
            pltpu.VMEM((2, MODES, 128), F32),
            pltpu.VMEM((64, 32, 128), BF16),
            pltpu.VMEM((CHUNKS, PER, 128), F32),
            pltpu.VMEM((CHUNKS, TOK, 128), BF16),
            pltpu.VMEM((CHUNKS, TOK, 256), BF16),
            pltpu.VMEM((CHUNKS, TOK, 256), F32),
            pltpu.VMEM((CHUNKS, PER, 128), F32),
            pltpu.VMEM((PLANE, 32, 128), BF16),
            pltpu.VMEM((PLANE, 32, 128), BF16),
            pltpu.VMEM((2, 8, 128), F32),
            pltpu.VMEM((PLANE, 8, 128), F32),
            pltpu.VMEM((24, 128), F32),
            pltpu.VMEM((24, 128), F32),
            pltpu.VMEM((PLANE, 8, 128), F32),
            pltpu.VMEM((PLANE, 8, 128), F32),
            pltpu.VMEM((PLANE, 32, 128), BF16),
            pltpu.VMEM((PLANE, 32, 128), BF16),
            pltpu.VMEM((MODES, 128), F32),
            pltpu.VMEM((8, MODES, 128), F32),
            dma((4,)),
            dma((2,)),
            dma((5,)),
            dma(()),
            dma(()),
            dma(()),
            dma(()),
            dma(()),
        ],
        compiler_params=pltpu.CompilerParams(
            collective_id=0, has_side_effects=True, vmem_limit_bytes=32 * 1024 * 1024
        ),
    )(query_rows, key_rows, value_rows, grad_rows, residues.T, decay_rates.T)
    op, gq, gk, gv, gres, grate = outs
    return op, gq, gk, gv, gres.T, grate.T


def solution(mesh):
    wide = P("ctx", "tensor")
    return jax.shard_map(
        per_device,
        mesh=mesh,
        in_specs=(wide, wide, wide, wide, P(), P()),
        out_specs=(wide, wide, wide, wide, P(), P()),
        check_vma=False,
    )
```

```python
import functools

import jax
import jax.numpy as jnp
from jax import lax
from jax.experimental import pallas as pl
from jax.experimental.pallas import tpu as pltpu
from jax.sharding import PartitionSpec as P

MESH = pl.DeviceIdType.MESH
F32 = jnp.float32
BF16 = jnp.bfloat16
EXACT = lax.Precision.HIGHEST

TOK = 128
CHUNKS = 8
PER = 8
GROUP = 16
MODES = 16
PLANE = 16


def iota(shape, dim):
    return lax.broadcasted_iota(jnp.int32, shape, dim)


def dot(a, b, precision=None):
    return lax.dot_general(
        a, b, (((1,), (0,)), ((), ())), precision=precision, preferred_element_type=F32
    )


def dot_nt(a, b):
    return lax.dot_general(a, b, (((1,), (1,)), ((), ())), preferred_element_type=F32)


def kernel(
    q_hbm, k_hbm, v_hbm, g_hbm, res_hbm, rate_hbm,
    op_hbm, gq_hbm, gk_hbm, gv_hbm, grads_hbm,
    op_ref, gq_ref, gk_ref, gv_ref,
    q_v, k_v, v_v, g_v, par, wst, hrev, acoef, rhs, local, lagrev,
    send1, recv1, across, gsend, grecv, fstate, send2, recv2, xsend, xrecv, ysend,
    in_sem, out_sem, par_sem, send_sem,
    recv1_sem, across_sem, recvg_sem, recv2_sem, recvx_sem, recvy_sem, own_sem,
):
    def arrived(ref, count, sem):
        pltpu.make_async_copy(ref.at[pl.ds(0, count)], ref.at[pl.ds(0, count)], sem).wait()

    ctx = lax.axis_index("ctx")
    tau = lax.axis_index("tensor")
    plane = ctx // PLANE
    me = ctx % PLANE
    base = plane * PLANE
    other = (1 - plane) * PLANE
    column = plane * 8 + tau

    def along_z(i):
        peer = (column + i) % 16
        return {"ctx": (peer // 8) * PLANE + me, "tensor": peer % 8}

    lanes = pl.ds(pl.multiple_of((tau // 2) * 128, 128), 128)
    par_copies = [
        pltpu.make_async_copy(res_hbm.at[:, lanes], par.at[0], par_sem.at[0]),
        pltpu.make_async_copy(rate_hbm.at[:, lanes], par.at[1], par_sem.at[1]),
    ]
    in_copies = [
        pltpu.make_async_copy(src, dst, in_sem.at[i])
        for i, (src, dst) in enumerate(((q_hbm, q_v), (k_hbm, k_v), (g_hbm, g_v), (v_hbm, v_v)))
    ]
    for copy in par_copies + in_copies:
        copy.start()

    barrier = pltpu.get_barrier_semaphore()

    @pl.loop(1, 2 * PLANE)
    def _(i):
        pl.semaphore_signal(
            barrier, inc=1, device_id={"ctx": (ctx + i) % (2 * PLANE)}, device_id_type=MESH
        )

    @pl.loop(1, 16)
    def _(i):
        pl.semaphore_signal(barrier, inc=1, device_id=along_z(i), device_id_type=MESH)

    for copy in par_copies:
        copy.wait()

    lane16 = iota((MODES, 128), 1)
    odd = (tau % 2) == 1

    def own_half(x):
        rolled = pltpu.roll(x, 64, 1)
        first = jnp.where(odd, rolled, x)
        return jnp.where(lane16 < 64, first, jnp.where(odd, x, rolled))

    res_t = own_half(par[0])
    rate_t = own_half(par[1])

    behind = (127 - lane16).astype(F32)
    ahead = (lane16 + 1).astype(F32)

    for k in range(CHUNKS):
        for i in range(PER):
            f = k * PER + i
            decay = jnp.exp(-rate_t[:, f : f + 1] * behind)
            wst[f, 0:16, :] = decay.astype(BF16)
            wst[f, 16:32, :] = (decay * behind).astype(BF16)

    for copy in in_copies:
        copy.wait()

    turn = (iota((TOK, TOK), 0) + iota((TOK, TOK), 1) == TOK - 1).astype(BF16)
    group_of = (iota((1, 256), 1) % 128) // GROUP

    for k in range(CHUNKS):
        cols = slice(128 * k, 128 * k + 128)
        rhs[k, :, 0:128] = (q_v[:, cols].astype(F32) * k_v[:, cols].astype(F32)).astype(BF16)
        dz = (g_v[:, cols].astype(F32) * v_v[:, cols].astype(F32)).astype(BF16)
        rhs[k, :, 128:256] = dot(turn, dz).astype(BF16)

    for k in range(CHUNKS):
        weights = wst[pl.ds(k * PER, PER)].reshape(PER * 32, TOK)
        ends = dot(weights, rhs[k])
        total = jnp.zeros((32, 256), F32)
        for i in range(PER):
            total = jnp.where(group_of == i, ends[32 * i : 32 * i + 32], total)
        for h in range(2):
            rows = slice(8 * h, 8 * h + 8)
            rows2 = slice(16 + 8 * h, 24 + 8 * h)
            send1[2 * k + h] = jnp.concatenate(
                [
                    total[rows, 0:128],
                    total[rows, 128:256],
                    total[rows2, 0:128],
                    total[rows2, 128:256],
                ],
                axis=0,
            ).astype(BF16)

    pl.semaphore_wait(barrier, 2 * PLANE - 1 + 15)

    @pl.loop(0, PLANE)
    def _(i):
        peer = (me + i) % PLANE
        pltpu.make_async_remote_copy(
            src_ref=send1.at[peer, pl.ds(0, 16)],
            dst_ref=across.at[me],
            send_sem=send_sem.at[2],
            recv_sem=across_sem,
            device_id={"ctx": other + peer},
            device_id_type=MESH,
        ).start()


    @pl.loop(1, PLANE)
    def _(i):
        peer = (me + i) % PLANE
        pltpu.make_async_remote_copy(
            src_ref=send1.at[peer],
            dst_ref=recv1.at[me],
            send_sem=send_sem.at[0],
            recv_sem=recv1_sem,
            device_id={"ctx": base + peer},
            device_id_type=MESH,
        ).start()

    recv1[me] = send1[me]

    row = iota((TOK, TOK), 0)
    lane = iota((TOK, TOK), 1)

    @pl.loop(0, CHUNKS, unroll=True)
    def _(k):
        u = rhs[k, :, 0:128]
        dz = rhs[k, :, 128:256]
        for i in range(PER):
            mine = jnp.where(group_of[:, 0:128] == i, dz, jnp.zeros_like(dz))
            pairs = dot_nt(mine, u)
            diag = pltpu.roll(pairs, 0, 1, stride=1, stride_axis=0)
            lagrev[k, i : i + 1, :] = jnp.sum(
                jnp.where(lane >= row, diag, 0.0), axis=0, keepdims=True
            )

    lag_all = lagrev[...].reshape(64, 128).astype(BF16)
    lag_all = jnp.concatenate([lag_all, lag_all], axis=0)
    lane_filter = iota((32, 128), 1)
    kind_filter = jnp.where(iota((32, 128), 0) < 16, lane_filter, lane_filter - 64)

    def add_filter(k, total):
        part = dot_nt(wst[pl.ds(k * PER, PER)].reshape(PER * 32, TOK), lag_all)
        for i in range(PER):
            total = jnp.where(kind_filter == k * PER + i, part[32 * i : 32 * i + 32], total)
        return total

    local_sums = lax.fori_loop(0, CHUNKS, add_filter, jnp.zeros((32, 128), F32), unroll=True)
    local_sums = local_sums[0:16] + local_sums[16:32]
    local_sums = jnp.where(lane16 < 64, local_sums, -res_t * local_sums)
    gsend[0] = local_sums[0:8]
    gsend[1] = local_sums[8:16]

    @pl.loop(1, PLANE)
    def _(i):
        peer = (me + i) % PLANE
        pltpu.make_async_remote_copy(
            src_ref=gsend.at[peer % 2],
            dst_ref=grecv.at[me],
            send_sem=send_sem.at[1],
            recv_sem=recvg_sem,
            device_id={"ctx": base + peer},
            device_id_type=MESH,
        ).start()

    grecv[me] = gsend[me % 2]

    for k in range(CHUNKS):
        powers = []
        for i in range(PER):
            f = k * PER + i
            rate = rate_t[:, f : f + 1]
            res = res_t[:, f : f + 1]
            decay = res * jnp.exp(-rate * behind)
            hrev[k, i : i + 1, :] = jnp.sum(decay, axis=0, keepdims=True)
            powers.append(res * jnp.exp(-rate * ahead))
        acoef[k] = jnp.concatenate(powers, axis=0).T.astype(BF16)

    @pl.loop(0, CHUNKS, unroll=True)
    def _(k):
        both = rhs[k]
        total = jnp.zeros((TOK, 256), F32)
        for i in range(PER):
            taps = pltpu.roll(
                jnp.broadcast_to(hrev[k, i : i + 1, :], (TOK, TOK)), 1, 1, stride=1, stride_axis=0
            )
            taps = jnp.where(lane <= row, taps, 0.0).astype(BF16)
            total = jnp.where(group_of == i, dot(taps, both), total)
        local[k] = total

    own_chunk = me // 2
    upper = (me % 2) == 1
    spread = (iota((128, 128), 0) == PER * own_chunk + iota((128, 128), 1) // GROUP).astype(F32)
    rate_spread = dot(rate_t, spread, EXACT)
    res_spread = dot(res_t, spread, EXACT)
    rate_own = jnp.where(upper, rate_spread[8:16], rate_spread[0:8])
    res_own = jnp.where(upper, res_spread[8:16], res_spread[0:8])
    step = jnp.exp(-rate_own * float(TOK))
    single = jnp.exp(-rate_own)
    collect = (iota((128, 128), 1) % 64 == 8 * tau + iota((128, 128), 0) // GROUP).astype(BF16)
    lane8 = iota((8, 128), 1)
    high = plane == 1

    arrived(recv1, PLANE - 1, recv1_sem)
    arrived(across, PLANE, across_sem)

    zero = jnp.zeros((8, 128), F32)
    incoming = zero
    for i in range(PLANE):
        block = across[jnp.where(high, i, PLANE - 1 - i)].astype(F32)
        incoming = step * incoming + jnp.where(high, block[0:8], block[8:16])
    forward = jnp.where(high, incoming, 0.0)
    backward = jnp.where(high, 0.0, incoming)
    for m in range(PLANE):
        fstate[m] = forward
        forward = step * forward + recv1[m, 0:16, :].astype(F32)[0:8]
    sum_one, sum_two, sum_mid = zero, zero, zero
    for m in reversed(range(PLANE)):
        block = recv1[m].astype(F32)
        start_one, end_two, start_two = block[8:16], block[16:24], block[24:32]
        forward = fstate[m]
        send2[m] = jnp.concatenate([forward, backward], axis=0).astype(BF16)
        sum_one = sum_one + forward * start_one
        sum_two = sum_two + (forward * start_two + end_two * backward)
        sum_mid = sum_mid + forward * backward
        backward = step * backward + start_one

    @pl.loop(1, PLANE)
    def _(i):
        peer = (me + i) % PLANE
        pltpu.make_async_remote_copy(
            src_ref=send2.at[peer],
            dst_ref=recv2.at[me],
            send_sem=send_sem.at[3],
            recv_sem=recv2_sem,
            device_id={"ctx": base + peer},
            device_id_type=MESH,
        ).start()

    sum_two = -res_own * single * (sum_two + sum_one + float(TOK) * step * sum_mid)
    sum_one = single * sum_one
    one_high, two_high = sum_one.astype(BF16), sum_two.astype(BF16)
    parts = jnp.concatenate(
        [
            one_high.astype(F32),
            sum_one - one_high.astype(F32),
            two_high.astype(F32),
            sum_two - two_high.astype(F32),
        ],
        axis=0,
    ).astype(BF16)
    parts = dot(parts, collect)
    grads = jnp.where(lane8 < 64, parts[0:8] + parts[8:16], parts[16:24] + parts[24:32])
    arrived(grecv, PLANE - 1, recvg_sem)
    inside = jnp.where((lane8 % 64) // PER == own_chunk, jnp.sum(grecv[...], axis=0), 0.0)
    grads = grads + pltpu.roll(inside, (128 + PER * (tau - own_chunk)) % 128, 1)
    xsend[...] = grads

    @pl.loop(1, 16)
    def _(i):
        pltpu.make_async_remote_copy(
            src_ref=xsend,
            dst_ref=xrecv.at[column],
            send_sem=send_sem.at[4],
            recv_sem=recvx_sem,
            device_id=along_z(i),
            device_id_type=MESH,
        ).start()

    xrecv[column] = grads
    recv2[me] = send2[me]

    arrived(xrecv, 15, recvx_sem)
    ysend[...] = jnp.sum(xrecv[...], axis=0)

    @pl.loop(1, PLANE)
    def _(i):
        pltpu.make_async_remote_copy(
            src_ref=ysend,
            dst_ref=grads_hbm.at[me],
            send_sem=send_sem.at[5],
            recv_sem=recvy_sem,
            device_id={"ctx": base + (me + i) % PLANE},
            device_id_type=MESH,
        ).start()

    own_copy = pltpu.make_async_copy(ysend, grads_hbm.at[me], own_sem)
    own_copy.start()

    arrived(recv2, PLANE - 1, recv2_sem)

    block_diagonal = (iota((PER, MODES, 256), 2) % 128) // GROUP == iota((PER, MODES, 256), 0)

    @pl.loop(0, CHUNKS, unroll=True)
    def _(k):
        cols = pl.ds(pl.multiple_of(k * 128, 128), 128)
        first = recv2[2 * k].astype(F32)
        second = recv2[2 * k + 1].astype(F32)
        states = jnp.concatenate(
            [
                jnp.concatenate([first[0:8], second[0:8]], axis=0),
                jnp.concatenate([first[8:16], second[8:16]], axis=0),
            ],
            axis=1,
        )
        states = jnp.where(block_diagonal, states[None], 0.0).reshape(PER * MODES, 256)
        total = local[k] + dot(acoef[k], states.astype(BF16))
        conv = total[:, 0:128].astype(BF16).astype(F32)
        back = dot(turn, total[:, 128:256].astype(BF16))
        op_ref[:, cols] = (v_v[:, cols].astype(F32) * conv).astype(BF16)
        gv_ref[:, cols] = (g_v[:, cols].astype(F32) * conv).astype(BF16)
        gq_ref[:, cols] = (k_v[:, cols].astype(F32) * back).astype(BF16)
        gk_ref[:, cols] = (q_v[:, cols].astype(F32) * back).astype(BF16)

    out_copies = [
        pltpu.make_async_copy(src, dst, out_sem.at[i])
        for i, (src, dst) in enumerate(
            ((op_ref, op_hbm), (gq_ref, gq_hbm), (gk_ref, gk_hbm), (gv_ref, gv_hbm))
        )
    ]
    for copy in out_copies:
        copy.start()

    arrived(send1, PLANE - 1, send_sem.at[0])
    arrived(grecv, PLANE - 1, send_sem.at[1])
    arrived(across, PLANE, send_sem.at[2])
    arrived(send2, PLANE - 1, send_sem.at[3])
    arrived(xrecv, 15, send_sem.at[4])
    arrived(xrecv, PLANE - 1, send_sem.at[5])
    own_copy.wait()
    for copy in out_copies:
        copy.wait()
    arrived(grads_hbm, PLANE - 1, recvy_sem)


def hand_over(
    op_in, gq_in, gk_in, gv_in, grads_in,
    op_out, gq_out, gk_out, gv_out, gres_ref, grate_ref,
    op_v, gq_v, gk_v, gv_v, grads_v, into_sem, out_sem,
):
    inputs = (op_in, gq_in, gk_in, gv_in)
    held = (op_v, gq_v, gk_v, gv_v)
    results = (op_out, gq_out, gk_out, gv_out)
    grads_copy = pltpu.make_async_copy(grads_in, grads_v, into_sem.at[4])
    into = [pltpu.make_async_copy(inputs[i], held[i], into_sem.at[i]) for i in range(4)]
    out = [pltpu.make_async_copy(held[i], results[i], out_sem.at[i]) for i in range(4)]
    grads_copy.start()
    for copy in into:
        copy.start()
    grads_copy.wait()

    lane = iota((MODES, 128), 1)
    rows = [
        jnp.concatenate([grads_v[2 * k], grads_v[2 * k + 1]], axis=0) for k in range(CHUNKS)
    ]
    for bit in (4, 2, 1):
        clear = (lane // PER) % (2 * bit) < bit
        turned = list(rows)
        for k in range(CHUNKS):
            if k & bit:
                continue
            near, far = rows[k], rows[k + bit]
            turned[k] = jnp.where(clear, near, pltpu.roll(far, PER * bit, 1))
            turned[k + bit] = jnp.where(clear, pltpu.roll(near, 128 - PER * bit, 1), far)
        rows = turned
    for j in range(4):
        even, uneven = rows[2 * j], rows[2 * j + 1]
        gres_ref[:, 128 * j : 128 * j + 128] = jnp.where(
            lane < 64, even, pltpu.roll(uneven, 64, 1)
        )
        grate_ref[:, 128 * j : 128 * j + 128] = jnp.where(
            lane < 64, pltpu.roll(even, 64, 1), uneven
        )

    for i in range(4):
        into[i].wait()
        out[i].start()
    for copy in out:
        copy.wait()


def per_device(query_rows, key_rows, value_rows, grad_rows, residues, decay_rates):
    rows, width = query_rows.shape
    any_spec = pl.BlockSpec(memory_space=pl.ANY)
    vmem_limit = 60 * 1024 * 1024
    wide = jax.ShapeDtypeStruct((rows, width), BF16)
    small = jax.ShapeDtypeStruct((MODES, 512), F32)
    dma = pltpu.SemaphoreType.DMA
    whole = pltpu.VMEM((rows, width), BF16)
    outs = pl.pallas_call(
        kernel,
        out_shape=(wide, wide, wide, wide, jax.ShapeDtypeStruct((PLANE, 8, 128), F32)),
        in_specs=[any_spec] * 6,
        out_specs=[any_spec] * 5,
        scratch_shapes=[whole] * 8
        + [
            pltpu.VMEM((2, MODES, 128), F32),
            pltpu.VMEM((64, 32, 128), BF16),
            pltpu.VMEM((CHUNKS, PER, 128), F32),
            pltpu.VMEM((CHUNKS, TOK, 128), BF16),
            pltpu.VMEM((CHUNKS, TOK, 256), BF16),
            pltpu.VMEM((CHUNKS, TOK, 256), F32),
            pltpu.VMEM((CHUNKS, PER, 128), F32),
            pltpu.VMEM((PLANE, 32, 128), BF16),
            pltpu.VMEM((PLANE, 32, 128), BF16),
            pltpu.VMEM((PLANE, 16, 128), BF16),
            pltpu.VMEM((2, 8, 128), F32),
            pltpu.VMEM((PLANE, 8, 128), F32),
            pltpu.VMEM((PLANE, 8, 128), F32),
            pltpu.VMEM((PLANE, 16, 128), BF16),
            pltpu.VMEM((PLANE, 16, 128), BF16),
            pltpu.VMEM((8, 128), F32),
            pltpu.VMEM((16, 8, 128), F32),
            pltpu.VMEM((8, 128), F32),
            dma((4,)),
            dma((4,)),
            dma((2,)),
            dma((6,)),
        ]
        + [dma(())] * 7,
        compiler_params=pltpu.CompilerParams(
            collective_id=0, has_side_effects=True, vmem_limit_bytes=vmem_limit
        ),
    )(query_rows, key_rows, value_rows, grad_rows, residues.T, decay_rates.T)
    vmem_spec = pl.BlockSpec(memory_space=pltpu.VMEM)
    op, gq, gk, gv, gres, grate = pl.pallas_call(
        hand_over,
        out_shape=(wide, wide, wide, wide, small, small),
        in_specs=[any_spec] * 5,
        out_specs=[any_spec] * 4 + [vmem_spec] * 2,
        scratch_shapes=[whole] * 4 + [pltpu.VMEM((PLANE, 8, 128), F32), dma((5,)), dma((4,))],
        compiler_params=pltpu.CompilerParams(vmem_limit_bytes=vmem_limit),
    )(*outs)
    return op, gq, gk, gv, gres.T, grate.T


def solution(mesh):
    wide = P("ctx", "tensor")
    return jax.shard_map(
        per_device,
        mesh=mesh,
        in_specs=(wide, wide, wide, wide, P(), P()),
        out_specs=(wide, wide, wide, wide, P(), P()),
        check_vma=False,
    )
```

```python
import functools

import jax
import jax.numpy as jnp
from jax import lax
from jax.experimental import pallas as pl
from jax.experimental.pallas import tpu as pltpu
from jax.sharding import PartitionSpec as P

MESH = pl.DeviceIdType.MESH
F32 = jnp.float32
BF16 = jnp.bfloat16
EXACT = lax.Precision.HIGHEST

TOK = 128
CHUNKS = 8
PER = 8
GROUP = 16
MODES = 16
PLANE = 16
FAR_FIRST = sorted(
    ((dx, dy) for dx in range(4) for dy in range(4) if dx or dy),
    key=lambda way: -(min(way[0], 4 - way[0]) + min(way[1], 4 - way[1])),
)


def iota(shape, dim):
    return lax.broadcasted_iota(jnp.int32, shape, dim)


def dot(a, b, precision=None):
    return lax.dot_general(
        a, b, (((1,), (0,)), ((), ())), precision=precision, preferred_element_type=F32
    )


def dot_nt(a, b):
    return lax.dot_general(a, b, (((1,), (1,)), ((), ())), preferred_element_type=F32)


def kernel(
    q_hbm, k_hbm, v_hbm, g_hbm, res_hbm, rate_hbm,
    op_ref, gq_ref, gk_ref, gv_ref, grads_ref,
    q_v, k_v, v_v, g_v, par, wst, hrev, acoef, rhs, local, lagrev,
    send1, recv1, gsend, grecv, tstate, ostate, zsend, zrecv, cross,
    send2, recv2, xsend, xrecv, ysend,
    in_sem, par_sem, send_sem,
    recv1_sem, recvg_sem, recvz_sem, recv2_sem, recvx_sem, recvy_sem, ready_sem,
):
    ctx = lax.axis_index("ctx")
    tau = lax.axis_index("tensor")
    plane = ctx // PLANE
    me = ctx % PLANE
    z = plane * 4 + tau // 2
    core = tau % 2
    base = plane * PLANE
    first = plane == 0
    second = plane == 1

    def arrived(ref, count, sem):
        pltpu.make_async_copy(ref.at[pl.ds(0, count)], ref.at[pl.ds(0, count)], sem).wait()

    def in_plane(offset):
        return base + ((me // 4 + offset[0]) % 4) * 4 + (me % 4 + offset[1]) % 4

    def send(src, dst, kind, recv_sem, device):
        pltpu.make_async_remote_copy(
            src_ref=src,
            dst_ref=dst,
            send_sem=send_sem.at[kind],
            recv_sem=recv_sem,
            device_id=device,
            device_id_type=MESH,
        ).start()

    def z_arrived():
        pltpu.make_async_copy(zrecv, zrecv, recvz_sem).wait()

    def signal(device):
        pl.semaphore_signal(barrier, inc=1, device_id=device, device_id_type=MESH)

    lanes = pl.ds(pl.multiple_of((tau // 2) * 128, 128), 128)
    par_copies = [
        pltpu.make_async_copy(res_hbm.at[:, lanes], par.at[0], par_sem.at[0]),
        pltpu.make_async_copy(rate_hbm.at[:, lanes], par.at[1], par_sem.at[1]),
    ]
    in_copies = [
        pltpu.make_async_copy(src, dst, in_sem.at[i])
        for i, (src, dst) in enumerate(((q_hbm, q_v), (k_hbm, k_v), (g_hbm, g_v), (v_hbm, v_v)))
    ]
    for copy in par_copies + in_copies:
        copy.start()

    barrier = pltpu.get_barrier_semaphore()

    @pl.loop(1, PLANE)
    def _(i):
        signal({"ctx": base + (me + i) % PLANE})

    @pl.loop(1, 8)
    def _(i):
        signal({"tensor": (tau + i) % 8})

    @pl.when(first)
    def _():
        @pl.loop(0, 8)
        def _(i):
            signal({"ctx": PLANE + me, "tensor": (tau + i) % 8})

    for copy in par_copies:
        copy.wait()

    lane16 = iota((MODES, 128), 1)
    odd = (tau % 2) == 1

    def own_half(x):
        rolled = pltpu.roll(x, 64, 1)
        first = jnp.where(odd, rolled, x)
        return jnp.where(lane16 < 64, first, jnp.where(odd, x, rolled))

    res_t = own_half(par[0])
    rate_t = own_half(par[1])

    behind = (127 - lane16).astype(F32)
    ahead = (lane16 + 1).astype(F32)

    for k in range(CHUNKS):
        for i in range(PER):
            f = k * PER + i
            decay = jnp.exp(-rate_t[:, f : f + 1] * behind)
            wst[f, 0:16, :] = decay.astype(BF16)
            wst[f, 16:32, :] = (decay * behind).astype(BF16)

    for copy in in_copies:
        copy.wait()

    turn = (iota((TOK, TOK), 0) + iota((TOK, TOK), 1) == TOK - 1).astype(BF16)
    group_of = (iota((1, 256), 1) % 128) // GROUP

    for k in range(CHUNKS):
        cols = slice(128 * k, 128 * k + 128)
        rhs[k, :, 0:128] = (q_v[:, cols].astype(F32) * k_v[:, cols].astype(F32)).astype(BF16)
        dz = (g_v[:, cols].astype(F32) * v_v[:, cols].astype(F32)).astype(BF16)
        rhs[k, :, 128:256] = dot(turn, dz).astype(BF16)

    for k in range(CHUNKS):
        weights = wst[pl.ds(k * PER, PER)].reshape(PER * 32, TOK)
        ends = dot(weights, rhs[k])
        total = jnp.zeros((32, 256), F32)
        for i in range(PER):
            total = jnp.where(group_of == i, ends[32 * i : 32 * i + 32], total)
        for h in range(2):
            rows = slice(8 * h, 8 * h + 8)
            rows2 = slice(16 + 8 * h, 24 + 8 * h)
            send1[2 * k + h] = jnp.concatenate(
                [
                    total[rows, 0:128],
                    total[rows, 128:256],
                    total[rows2, 0:128],
                    total[rows2, 128:256],
                ],
                axis=0,
            ).astype(BF16)

    @pl.when(first)
    def _():
        pl.semaphore_wait(barrier, PLANE - 1 + 7)

    @pl.when(second)
    def _():
        pl.semaphore_wait(barrier, PLANE - 1 + 7 + 8)

        @pl.loop(0, 8)
        def _(i):
            pl.semaphore_signal(
                ready_sem,
                inc=1,
                device_id={"ctx": me, "tensor": (tau + i) % 8},
                device_id_type=MESH,
            )

    for offset in FAR_FIRST:
        peer = in_plane(offset)
        send(send1.at[peer - base], recv1.at[me], 0, recv1_sem, {"ctx": peer})
    recv1[me] = send1[me]

    row = iota((TOK, TOK), 0)
    lane = iota((TOK, TOK), 1)

    @pl.loop(0, CHUNKS, unroll=True)
    def _(k):
        u = rhs[k, :, 0:128]
        dz = rhs[k, :, 128:256]
        for i in range(PER):
            mine = jnp.where(group_of[:, 0:128] == i, dz, jnp.zeros_like(dz))
            pairs = dot_nt(mine, u)
            diag = pltpu.roll(pairs, 0, 1, stride=1, stride_axis=0)
            lagrev[k, i : i + 1, :] = jnp.sum(
                jnp.where(lane >= row, diag, 0.0), axis=0, keepdims=True
            )

    lag_all = lagrev[...].reshape(64, 128).astype(BF16)
    lag_all = jnp.concatenate([lag_all, lag_all], axis=0)
    lane_filter = iota((32, 128), 1)
    kind_filter = jnp.where(iota((32, 128), 0) < 16, lane_filter, lane_filter - 64)

    def add_filter(k, total):
        part = dot_nt(wst[pl.ds(k * PER, PER)].reshape(PER * 32, TOK), lag_all)
        for i in range(PER):
            total = jnp.where(kind_filter == k * PER + i, part[32 * i : 32 * i + 32], total)
        return total

    local_sums = lax.fori_loop(0, CHUNKS, add_filter, jnp.zeros((32, 128), F32), unroll=True)
    local_sums = local_sums[0:16] + local_sums[16:32]
    local_sums = jnp.where(lane16 < 64, local_sums, -res_t * local_sums)
    gsend[0] = local_sums[0:8]
    gsend[1] = local_sums[8:16]

    for offset in FAR_FIRST:
        peer = in_plane(offset)
        send(gsend.at[peer % 2], grecv.at[me], 1, recvg_sem, {"ctx": peer})
    grecv[me] = gsend[me % 2]

    for k in range(CHUNKS):
        powers = []
        for i in range(PER):
            f = k * PER + i
            rate = rate_t[:, f : f + 1]
            res = res_t[:, f : f + 1]
            decay = res * jnp.exp(-rate * behind)
            hrev[k, i : i + 1, :] = jnp.sum(decay, axis=0, keepdims=True)
            powers.append(res * jnp.exp(-rate * ahead))
        acoef[k] = jnp.concatenate(powers, axis=0).T.astype(BF16)

    @pl.loop(0, CHUNKS, unroll=True)
    def _(k):
        both = rhs[k]
        total = jnp.zeros((TOK, 256), F32)
        for i in range(PER):
            taps = pltpu.roll(
                jnp.broadcast_to(hrev[k, i : i + 1, :], (TOK, TOK)), 1, 1, stride=1, stride_axis=0
            )
            taps = jnp.where(lane <= row, taps, 0.0).astype(BF16)
            total = jnp.where(group_of == i, dot(taps, both), total)
        local[k] = total

    own_chunk = me // 2
    upper = (me % 2) == 1
    spread = (iota((128, 128), 0) == PER * own_chunk + iota((128, 128), 1) // GROUP).astype(F32)
    rate_spread = dot(rate_t, spread, EXACT)
    res_spread = dot(res_t, spread, EXACT)
    rate_own = jnp.where(upper, rate_spread[8:16], rate_spread[0:8])
    res_own = jnp.where(upper, res_spread[8:16], res_spread[0:8])
    step = jnp.exp(-rate_own * float(TOK))
    single = jnp.exp(-rate_own)
    collect = (iota((128, 128), 1) % 64 == 8 * tau + iota((128, 128), 0) // GROUP).astype(BF16)
    lane8 = iota((8, 128), 1)
    zero = jnp.zeros((8, 128), F32)

    arrived(recv1, PLANE - 1, recv1_sem)

    def place(i):
        return jnp.where(first, i, PLANE - 1 - i)

    away_ends = []
    one, two, sum_one, sum_two = zero, zero, zero, zero
    for i in range(PLANE):
        block = recv1[place(i)].astype(F32)
        toward_one = jnp.where(first, block[0:8], block[8:16])
        away_one = jnp.where(first, block[8:16], block[0:8])
        toward_two = jnp.where(first, block[16:24], block[24:32])
        away_two = jnp.where(first, block[24:32], block[16:24])
        away_ends.append(away_one)
        tstate[i] = one
        sum_one = sum_one + one * away_one
        sum_two = sum_two + (two * away_one + one * (away_two + away_one))
        two = step * (two + float(TOK) * one) + toward_two
        one = step * one + toward_one
    zsend[0:8] = one
    zsend[8:16] = two
    partner = {"ctx": (1 - plane) * PLANE + me}

    @pl.when(first)
    def _():
        pl.semaphore_wait(ready_sem, 8)

    send(zsend, zrecv, 3, recvz_sem, partner)

    away = zero
    for i in reversed(range(PLANE)):
        ostate[i] = away
        away = step * away + away_ends[i]

    @pl.when(first)
    def _():
        cross[...] = jnp.zeros((16, 128), F32)

    @pl.when(second)
    def _():
        z_arrived()
        other_one, other_two = zrecv[0:8], zrecv[8:16]
        cross[0:8] = one * other_one
        cross[8:16] = two * other_one + one * (other_two + other_one)

    sum_one = single * (sum_one + cross[0:8])
    sum_two = -res_own * single * (sum_two + cross[8:16])
    one_high, two_high = sum_one.astype(BF16), sum_two.astype(BF16)
    parts = jnp.concatenate(
        [
            one_high.astype(F32),
            sum_one - one_high.astype(F32),
            two_high.astype(F32),
            sum_two - two_high.astype(F32),
        ],
        axis=0,
    ).astype(BF16)
    parts = dot(parts, collect)
    grads = jnp.where(lane8 < 64, parts[0:8] + parts[8:16], parts[16:24] + parts[24:32])
    arrived(grecv, PLANE - 1, recvg_sem)
    inside = jnp.where((lane8 % 64) // PER == own_chunk, jnp.sum(grecv[...], axis=0), 0.0)
    grads = grads + pltpu.roll(inside, (128 + PER * (tau - own_chunk)) % 128, 1)
    xsend[...] = grads
    xrecv[plane * 8 + tau] = grads

    for hop in (4, 3, 5, 2, 6, 1, 7, 0):
        there = (z + hop) % 8
        for other in (1 - core, core) if hop else (1 - core,):
            device = {"ctx": (there // 4) * PLANE + me, "tensor": (there % 4) * 2 + other}
            send(xsend, xrecv.at[plane * 8 + tau], 4, recvx_sem, device)

    @pl.when(first)
    def _():
        z_arrived()

    passed = zrecv[0:8]
    for i in reversed(range(PLANE)):
        away = ostate[i] + passed
        send2[place(i)] = jnp.concatenate(
            [jnp.where(first, tstate[i], away), jnp.where(first, away, tstate[i])], axis=0
        ).astype(BF16)
        passed = step * passed
    for offset in FAR_FIRST:
        peer = in_plane(offset)
        send(send2.at[peer - base], recv2.at[me], 2, recv2_sem, {"ctx": peer})
    recv2[me] = send2[me]

    arrived(xrecv, 15, recvx_sem)
    total = jnp.sum(xrecv[...], axis=0)
    ysend[...] = total
    for offset in FAR_FIRST:
        send(ysend, grads_ref.at[me], 5, recvy_sem, {"ctx": in_plane(offset)})
    grads_ref[me] = total

    arrived(recv2, PLANE - 1, recv2_sem)

    block_diagonal = (iota((PER, MODES, 256), 2) % 128) // GROUP == iota((PER, MODES, 256), 0)

    @pl.loop(0, CHUNKS, unroll=True)
    def _(k):
        cols = pl.ds(pl.multiple_of(k * 128, 128), 128)
        first = recv2[2 * k].astype(F32)
        second = recv2[2 * k + 1].astype(F32)
        states = jnp.concatenate(
            [
                jnp.concatenate([first[0:8], second[0:8]], axis=0),
                jnp.concatenate([first[8:16], second[8:16]], axis=0),
            ],
            axis=1,
        )
        states = jnp.where(block_diagonal, states[None], 0.0).reshape(PER * MODES, 256)
        total = local[k] + dot(acoef[k], states.astype(BF16))
        conv = total[:, 0:128].astype(BF16).astype(F32)
        back = dot(turn, total[:, 128:256].astype(BF16))
        op_ref[:, cols] = (v_v[:, cols].astype(F32) * conv).astype(BF16)
        gv_ref[:, cols] = (g_v[:, cols].astype(F32) * conv).astype(BF16)
        gq_ref[:, cols] = (k_v[:, cols].astype(F32) * back).astype(BF16)
        gk_ref[:, cols] = (q_v[:, cols].astype(F32) * back).astype(BF16)

    arrived(send1, PLANE - 1, send_sem.at[0])
    arrived(grecv, PLANE - 1, send_sem.at[1])
    arrived(send2, PLANE - 1, send_sem.at[2])
    pltpu.make_async_copy(zsend, zsend, send_sem.at[3]).wait()
    arrived(xrecv, 15, send_sem.at[4])
    arrived(grads_ref, PLANE - 1, send_sem.at[5])
    arrived(grads_ref, PLANE - 1, recvy_sem)


def hand_over(
    op_v, gq_v, gk_v, gv_v, grads_v,
    op_out, gq_out, gk_out, gv_out, gres_out, grate_out,
    gres_v, grate_v, out_sem,
):
    held = (op_v, gq_v, gk_v, gv_v, gres_v, grate_v)
    results = (op_out, gq_out, gk_out, gv_out, gres_out, grate_out)
    out = [pltpu.make_async_copy(held[i], results[i], out_sem.at[i]) for i in range(6)]
    for copy in out[:4]:
        copy.start()

    lane = iota((MODES, 128), 1)
    rows = [
        jnp.concatenate([grads_v[2 * k], grads_v[2 * k + 1]], axis=0) for k in range(CHUNKS)
    ]
    for bit in (4, 2, 1):
        clear = (lane // PER) % (2 * bit) < bit
        turned = list(rows)
        for k in range(CHUNKS):
            if k & bit:
                continue
            near, far = rows[k], rows[k + bit]
            turned[k] = jnp.where(clear, near, pltpu.roll(far, PER * bit, 1))
            turned[k + bit] = jnp.where(clear, pltpu.roll(near, 128 - PER * bit, 1), far)
        rows = turned
    for j in range(4):
        even, uneven = rows[2 * j], rows[2 * j + 1]
        gres_v[:, 128 * j : 128 * j + 128] = jnp.where(
            lane < 64, even, pltpu.roll(uneven, 64, 1)
        )
        grate_v[:, 128 * j : 128 * j + 128] = jnp.where(
            lane < 64, pltpu.roll(even, 64, 1), uneven
        )
    out[4].start()
    out[5].start()

    for copy in out:
        copy.wait()


def per_device(query_rows, key_rows, value_rows, grad_rows, residues, decay_rates):
    rows, width = query_rows.shape
    any_spec = pl.BlockSpec(memory_space=pl.ANY)
    vmem_spec = pl.BlockSpec(memory_space=pltpu.VMEM)
    vmem_limit = 16 * 1024 * 1024
    wide = jax.ShapeDtypeStruct((rows, width), BF16)
    small = jax.ShapeDtypeStruct((MODES, 512), F32)
    dma = pltpu.SemaphoreType.DMA
    whole = pltpu.VMEM((rows, width), BF16)
    outs = pl.pallas_call(
        kernel,
        out_shape=(whole, whole, whole, whole, pltpu.VMEM((PLANE, 8, 128), F32)),
        in_specs=[any_spec] * 6,
        out_specs=[vmem_spec] * 5,
        scratch_shapes=[whole] * 4
        + [
            pltpu.VMEM((2, MODES, 128), F32),
            pltpu.VMEM((64, 32, 128), BF16),
            pltpu.VMEM((CHUNKS, PER, 128), F32),
            pltpu.VMEM((CHUNKS, TOK, 128), BF16),
            pltpu.VMEM((CHUNKS, TOK, 256), BF16),
            pltpu.VMEM((CHUNKS, TOK, 256), F32),
            pltpu.VMEM((CHUNKS, PER, 128), F32),
            pltpu.VMEM((PLANE, 32, 128), BF16),
            pltpu.VMEM((PLANE, 32, 128), BF16),
            pltpu.VMEM((2, 8, 128), F32),
            pltpu.VMEM((PLANE, 8, 128), F32),
            pltpu.VMEM((PLANE, 8, 128), F32),
            pltpu.VMEM((PLANE, 8, 128), F32),
            pltpu.VMEM((16, 128), F32),
            pltpu.VMEM((16, 128), F32),
            pltpu.VMEM((16, 128), F32),
            pltpu.VMEM((PLANE, 16, 128), BF16),
            pltpu.VMEM((PLANE, 16, 128), BF16),
            pltpu.VMEM((8, 128), F32),
            pltpu.VMEM((16, 8, 128), F32),
            pltpu.VMEM((8, 128), F32),
            dma((4,)),
            dma((2,)),
            dma((6,)),
        ]
        + [dma(())] * 6
        + [pltpu.SemaphoreType.REGULAR],
        compiler_params=pltpu.CompilerParams(
            collective_id=0, has_side_effects=True, vmem_limit_bytes=vmem_limit
        ),
    )(
        *(
            pltpu.with_memory_space_constraint(x, pltpu.HBM)
            for x in (query_rows, key_rows, value_rows, grad_rows, residues.T, decay_rates.T)
        )
    )
    op, gq, gk, gv, gres, grate = pl.pallas_call(
        hand_over,
        out_shape=(wide, wide, wide, wide, small, small),
        in_specs=[vmem_spec] * 5,
        out_specs=[any_spec] * 6,
        scratch_shapes=[pltpu.VMEM((MODES, 512), F32)] * 2 + [dma((6,))],
        compiler_params=pltpu.CompilerParams(vmem_limit_bytes=vmem_limit),
    )(*outs)
    return op, gq, gk, gv, gres.T, grate.T


def solution(mesh):
    wide = P("ctx", "tensor")
    return jax.shard_map(
        per_device,
        mesh=mesh,
        in_specs=(wide, wide, wide, wide, P(), P()),
        out_specs=(wide, wide, wide, wide, P(), P()),
        check_vma=False,
    )
```

```python
import functools

import jax
import jax.numpy as jnp
from jax import lax
from jax.experimental import pallas as pl
from jax.experimental.pallas import tpu as pltpu
from jax.sharding import PartitionSpec as P

MESH = pl.DeviceIdType.MESH
F32 = jnp.float32
BF16 = jnp.bfloat16
EXACT = lax.Precision.HIGHEST

TOK = 128
CHUNKS = 8
PER = 8
GROUP = 16
MODES = 16
PLANE = 16
OWNERS = [4 * (k // 3) + k % 3 for k in range(CHUNKS)]
EARLY_FIRST = sorted(range(PLANE), key=lambda spot: spot // 4 + spot % 4)


def iota(shape, dim):
    return lax.broadcasted_iota(jnp.int32, shape, dim)


def dot(a, b, precision=None):
    return lax.dot_general(
        a, b, (((1,), (0,)), ((), ())), precision=precision, preferred_element_type=F32
    )


def dot_nt(a, b):
    return lax.dot_general(a, b, (((1,), (1,)), ((), ())), preferred_element_type=F32)


def kernel(
    q_hbm, k_hbm, v_hbm, g_hbm, res_hbm, rate_hbm,
    op_ref, gq_ref, gk_ref, gv_ref, grads_ref,
    q_v, k_v, v_v, g_v, par, wst, hrev, acoef, rhs, local, lagrev,
    send1, recv1, gsend, grecv, zsend, zrecv, wsend, wrecv, passing,
    send2, recv2, xsend, xrecv, ysend,
    in_sem, par_sem, send_sem,
    recv1_sem, recvg_sem, recvz_sem, recvw_sem, recv2_sem, recvx_sem, recvy_sem, ready_sem,
):
    ctx = lax.axis_index("ctx")
    tau = lax.axis_index("tensor")
    plane = ctx // PLANE
    me = ctx % PLANE
    z = plane * 4 + tau // 2
    core = tau % 2
    base = plane * PLANE
    first = plane == 0
    second = plane == 1
    x, y = me // 4, me % 4
    own_chunk = 3 * x + y
    owner = jnp.logical_and(jnp.logical_and(x < 3, y < 3), own_chunk < CHUNKS)
    plain = jnp.logical_not(owner)
    first_owner = jnp.logical_and(first, owner)
    second_owner = jnp.logical_and(second, owner)

    def arrived(ref, count, sem):
        pltpu.make_async_copy(ref.at[pl.ds(0, count)], ref.at[pl.ds(0, count)], sem).wait()

    def arrived_from_owners(ref, sem):
        @pl.when(owner)
        def _():
            arrived(ref, CHUNKS - 1, sem)

        @pl.when(plain)
        def _():
            arrived(ref, CHUNKS, sem)

    def send(src, dst, kind, recv_sem, device):
        pltpu.make_async_remote_copy(
            src_ref=src,
            dst_ref=dst,
            send_sem=send_sem.at[kind],
            recv_sem=recv_sem,
            device_id=device,
            device_id_type=MESH,
        ).start()

    def signal(device):
        pl.semaphore_signal(barrier, inc=1, device_id=device, device_id_type=MESH)

    barrier = pltpu.get_barrier_semaphore()

    @pl.when(owner)
    def _():
        @pl.loop(1, PLANE)
        def _(i):
            signal({"ctx": base + (me + i) % PLANE})

        @pl.loop(1, 8)
        def _(i):
            signal({"tensor": (tau + i) % 8})

    @pl.when(first_owner)
    def _():
        @pl.loop(0, 8)
        def _(i):
            signal({"ctx": PLANE + me, "tensor": (tau + i) % 8})

    lanes = pl.ds(pl.multiple_of((tau // 2) * 128, 128), 128)
    par_copies = [
        pltpu.make_async_copy(res_hbm.at[:, lanes], par.at[0], par_sem.at[0]),
        pltpu.make_async_copy(rate_hbm.at[:, lanes], par.at[1], par_sem.at[1]),
    ]
    in_copies = [
        pltpu.make_async_copy(src, dst, in_sem.at[i])
        for i, (src, dst) in enumerate(((q_hbm, q_v), (k_hbm, k_v), (g_hbm, g_v), (v_hbm, v_v)))
    ]
    for copy in par_copies + in_copies:
        copy.start()

    for copy in par_copies:
        copy.wait()

    lane16 = iota((MODES, 128), 1)
    odd = (tau % 2) == 1

    def own_half(x):
        rolled = pltpu.roll(x, 64, 1)
        first = jnp.where(odd, rolled, x)
        return jnp.where(lane16 < 64, first, jnp.where(odd, x, rolled))

    res_t = own_half(par[0])
    rate_t = own_half(par[1])

    behind = (127 - lane16).astype(F32)
    ahead = (lane16 + 1).astype(F32)

    for k in range(CHUNKS):
        for i in range(PER):
            f = k * PER + i
            decay = jnp.exp(-rate_t[:, f : f + 1] * behind)
            wst[f, 0:16, :] = decay.astype(BF16)
            wst[f, 16:32, :] = (decay * behind).astype(BF16)

    for copy in in_copies:
        copy.wait()

    turn = (iota((TOK, TOK), 0) + iota((TOK, TOK), 1) == TOK - 1).astype(BF16)
    group_of = (iota((1, 256), 1) % 128) // GROUP

    for k in range(CHUNKS):
        cols = slice(128 * k, 128 * k + 128)
        rhs[k, :, 0:128] = (q_v[:, cols].astype(F32) * k_v[:, cols].astype(F32)).astype(BF16)
        dz = (g_v[:, cols].astype(F32) * v_v[:, cols].astype(F32)).astype(BF16)
        rhs[k, :, 128:256] = dot(turn, dz).astype(BF16)

    for k in range(CHUNKS):
        weights = wst[pl.ds(k * PER, PER)].reshape(PER * 32, TOK)
        ends = dot(weights, rhs[k])
        total = jnp.zeros((32, 256), F32)
        for i in range(PER):
            total = jnp.where(group_of == i, ends[32 * i : 32 * i + 32], total)
        toward = jnp.where(first, total[:, 0:128], total[:, 128:256])
        away = jnp.where(first, total[:, 128:256], total[:, 0:128])
        send1[k] = jnp.concatenate(
            [toward[0:16], away[0:16], toward[16:32], away[16:32]], axis=0
        ).astype(BF16)

    @pl.when(plain)
    def _():
        pl.semaphore_wait(barrier, CHUNKS)

    @pl.when(first_owner)
    def _():
        pl.semaphore_wait(barrier, CHUNKS - 1 + 7)

    partner = {"ctx": (1 - plane) * PLANE + me}

    @pl.when(second_owner)
    def _():
        pl.semaphore_wait(barrier, CHUNKS - 1 + 7 + 8)

        @pl.loop(0, 8)
        def _(i):
            pl.semaphore_signal(
                ready_sem,
                inc=1,
                device_id={"ctx": me, "tensor": (tau + i) % 8},
                device_id_type=MESH,
            )

    def place(m):
        return jnp.where(first, m, PLANE - 1 - m)

    for k, peer in enumerate(OWNERS):

        @pl.when(me != peer)
        def _():
            send(send1.at[k], recv1.at[place(me)], 0, recv1_sem, {"ctx": base + peer})

        @pl.when(me == peer)
        def _():
            recv1[place(me)] = send1[k]

    row = iota((TOK, TOK), 0)
    lane = iota((TOK, TOK), 1)

    @pl.loop(0, CHUNKS, unroll=True)
    def _(k):
        u = rhs[k, :, 0:128]
        dz = rhs[k, :, 128:256]
        for i in range(PER):
            mine = jnp.where(group_of[:, 0:128] == i, dz, jnp.zeros_like(dz))
            pairs = dot_nt(mine, u)
            diag = pltpu.roll(pairs, 0, 1, stride=1, stride_axis=0)
            lagrev[k, i : i + 1, :] = jnp.sum(
                jnp.where(lane >= row, diag, 0.0), axis=0, keepdims=True
            )

    lag_all = lagrev[...].reshape(64, 128).astype(BF16)
    lag_all = jnp.concatenate([lag_all, lag_all], axis=0)
    lane_filter = iota((32, 128), 1)
    kind_filter = jnp.where(iota((32, 128), 0) < 16, lane_filter, lane_filter - 64)

    def add_filter(k, total):
        part = dot_nt(wst[pl.ds(k * PER, PER)].reshape(PER * 32, TOK), lag_all)
        for i in range(PER):
            total = jnp.where(kind_filter == k * PER + i, part[32 * i : 32 * i + 32], total)
        return total

    local_sums = lax.fori_loop(0, CHUNKS, add_filter, jnp.zeros((32, 128), F32), unroll=True)
    local_sums = local_sums[0:16] + local_sums[16:32]
    local_sums = jnp.where(lane16 < 64, local_sums, -res_t * local_sums)
    gsend[...] = local_sums
    for peer in OWNERS:

        @pl.when(me != peer)
        def _():
            send(gsend, grecv.at[me], 1, recvg_sem, {"ctx": base + peer})

    @pl.when(owner)
    def _():
        grecv[me] = gsend[...]

    for k in range(CHUNKS):
        powers = []
        for i in range(PER):
            f = k * PER + i
            rate = rate_t[:, f : f + 1]
            res = res_t[:, f : f + 1]
            decay = res * jnp.exp(-rate * behind)
            hrev[k, i : i + 1, :] = jnp.sum(decay, axis=0, keepdims=True)
            powers.append(res * jnp.exp(-rate * ahead))
        acoef[k] = jnp.concatenate(powers, axis=0).T.astype(BF16)

    @pl.loop(0, CHUNKS, unroll=True)
    def _(k):
        both = rhs[k]
        total = jnp.zeros((TOK, 256), F32)
        for i in range(PER):
            taps = pltpu.roll(
                jnp.broadcast_to(hrev[k, i : i + 1, :], (TOK, TOK)), 1, 1, stride=1, stride_axis=0
            )
            taps = jnp.where(lane <= row, taps, 0.0).astype(BF16)
            total = jnp.where(group_of == i, dot(taps, both), total)
        local[k] = total

    @pl.when(owner)
    def _():
        spread = (iota((128, 128), 0) == PER * own_chunk + iota((128, 128), 1) // GROUP).astype(F32)
        rate_spread = dot(rate_t, spread, EXACT)
        res_spread = dot(res_t, spread, EXACT)
        step = jnp.exp(-rate_spread * float(TOK))
        single = jnp.exp(-rate_spread)
        collect = (iota((128, 128), 1) % 64 == 8 * tau + iota((128, 128), 0) // GROUP).astype(BF16)
        zero = jnp.zeros((MODES, 128), F32)

        arrived(recv1, PLANE - 1, recv1_sem)

        away_ends, states = [], []
        one, two, sum_one, sum_two = zero, zero, zero, zero
        lag = float(TOK) * step
        for i in range(PLANE):
            block = recv1[i].astype(F32)
            toward_one, away_one, toward_two, away_two = (
                block[16 * part : 16 * part + 16] for part in range(4)
            )
            away_ends.append(away_one)
            states.append(one)
            sum_one = sum_one + one * away_one
            sum_two = sum_two + (two * away_one + one * (away_two + away_one))
            two = step * two + (lag * one + toward_two)
            one = step * one + toward_one

        def collected(one_sum, two_sum):
            one_sum, two_sum = single * one_sum, -res_spread * single * two_sum
            one_high, two_high = one_sum.astype(BF16), two_sum.astype(BF16)
            parts = jnp.concatenate(
                [
                    one_high.astype(F32),
                    one_sum - one_high.astype(F32),
                    two_high.astype(F32),
                    two_sum - two_high.astype(F32),
                ],
                axis=0,
            ).astype(BF16)
            parts = dot(parts, collect)
            return jnp.where(lane16 < 64, parts[0:16] + parts[16:32], parts[32:48] + parts[48:64])

        def within_plane():
            arrived(grecv, PLANE - 1, recvg_sem)
            inside = jnp.where((lane16 % 64) // PER == own_chunk, jnp.sum(grecv[...], axis=0), 0.0)
            inside = pltpu.roll(inside, (128 + PER * (tau - own_chunk)) % 128, 1)
            return inside + collected(sum_one, sum_two)

        def send_along_z(grads):
            xsend[...] = grads.astype(BF16)
            for there in range(8):
                for other in (1, 0):
                    device = {"ctx": (there // 4) * PLANE + me, "tensor": (there % 4) * 2 + other}

                    @pl.when(jnp.logical_or(z != there, core != other))
                    def _():
                        send(xsend, xrecv.at[plane * 8 + tau], 4, recvx_sem, device)

            xrecv[plane * 8 + tau] = grads.astype(BF16)

        @pl.when(first)
        def _():
            zsend[0:16] = one
            zsend[16:32] = two
            pl.semaphore_wait(ready_sem, 8)
            send(zsend, zrecv, 3, recvz_sem, partner)
            send_along_z(within_plane())

        @pl.when(second)
        def _():
            wsend[...] = one
            send(wsend, wrecv, 3, recvw_sem, partner)
            grads = within_plane()
            pltpu.make_async_copy(zrecv, zrecv, recvz_sem).wait()
            other_one, other_two = zrecv[0:16], zrecv[16:32]
            passing[...] = other_one
            send_along_z(
                grads
                + collected(one * other_one, two * other_one + one * (other_two + other_one))
            )

        @pl.when(first)
        def _():
            pltpu.make_async_copy(wrecv, wrecv, recvw_sem).wait()
            passing[...] = wrecv[...]

        passed = passing[...]
        away = zero
        for i in reversed(range(PLANE)):
            toward, beside = states[i], away + passed
            send2[i] = jnp.concatenate(
                [jnp.where(first, toward, beside), jnp.where(first, beside, toward)], axis=0
            ).astype(BF16)
            away = step * away + away_ends[i]
            passed = step * passed
        for peer in EARLY_FIRST:

            @pl.when(me != peer)
            def _():
                send(send2.at[place(peer)], recv2.at[own_chunk], 2, recv2_sem, {"ctx": base + peer})

        recv2[own_chunk] = send2[place(me)]

        arrived(xrecv, 15, recvx_sem)
        total = jnp.sum(xrecv[...].astype(F32), axis=0).astype(BF16)
        ysend[...] = total
        for peer in EARLY_FIRST:

            @pl.when(me != peer)
            def _():
                send(ysend, grads_ref.at[own_chunk], 5, recvy_sem, {"ctx": base + peer})

        grads_ref[own_chunk] = total

    arrived_from_owners(recv2, recv2_sem)

    block_diagonal = (iota((PER, MODES, 256), 2) % 128) // GROUP == iota((PER, MODES, 256), 0)

    @pl.loop(0, CHUNKS, unroll=True)
    def _(k):
        cols = pl.ds(pl.multiple_of(k * 128, 128), 128)
        block = recv2[k]
        states = jnp.concatenate([block[0:16], block[16:32]], axis=1).astype(F32)
        states = jnp.where(block_diagonal, states[None], 0.0).reshape(PER * MODES, 256)
        total = local[k] + dot(acoef[k], states.astype(BF16))
        conv = total[:, 0:128].astype(BF16).astype(F32)
        back = dot(turn, total[:, 128:256].astype(BF16))
        op_ref[:, cols] = (v_v[:, cols].astype(F32) * conv).astype(BF16)
        gv_ref[:, cols] = (g_v[:, cols].astype(F32) * conv).astype(BF16)
        gq_ref[:, cols] = (k_v[:, cols].astype(F32) * back).astype(BF16)
        gk_ref[:, cols] = (q_v[:, cols].astype(F32) * back).astype(BF16)

    arrived_from_owners(send1, send_sem.at[0])
    arrived_from_owners(grecv, send_sem.at[1])

    @pl.when(first_owner)
    def _():
        pltpu.make_async_copy(zsend, zsend, send_sem.at[3]).wait()

    @pl.when(second_owner)
    def _():
        pltpu.make_async_copy(wsend, wsend, send_sem.at[3]).wait()

    @pl.when(owner)
    def _():
        arrived(send2, PLANE - 1, send_sem.at[2])
        arrived(xrecv, 15, send_sem.at[4])
        arrived(xrecv, PLANE - 1, send_sem.at[5])

    arrived_from_owners(grads_ref, recvy_sem)


def hand_over(
    op_v, gq_v, gk_v, gv_v, grads_v,
    op_out, gq_out, gk_out, gv_out, gres_out, grate_out,
    gres_v, grate_v, out_sem,
):
    held = (op_v, gq_v, gk_v, gv_v, gres_v, grate_v)
    results = (op_out, gq_out, gk_out, gv_out, gres_out, grate_out)
    out = [pltpu.make_async_copy(held[i], results[i], out_sem.at[i]) for i in range(6)]
    for copy in out[:4]:
        copy.start()

    lane = iota((MODES, 128), 1)
    rows = [
        grads_v[k].astype(F32) for k in range(CHUNKS)
    ]
    for bit in (4, 2, 1):
        clear = (lane // PER) % (2 * bit) < bit
        turned = list(rows)
        for k in range(CHUNKS):
            if k & bit:
                continue
            near, far = rows[k], rows[k + bit]
            turned[k] = jnp.where(clear, near, pltpu.roll(far, PER * bit, 1))
            turned[k + bit] = jnp.where(clear, pltpu.roll(near, 128 - PER * bit, 1), far)
        rows = turned
    for j in range(4):
        even, uneven = rows[2 * j], rows[2 * j + 1]
        gres_v[:, 128 * j : 128 * j + 128] = jnp.where(
            lane < 64, even, pltpu.roll(uneven, 64, 1)
        )
        grate_v[:, 128 * j : 128 * j + 128] = jnp.where(
            lane < 64, pltpu.roll(even, 64, 1), uneven
        )
    out[4].start()
    out[5].start()

    for copy in out:
        copy.wait()


def per_device(query_rows, key_rows, value_rows, grad_rows, residues, decay_rates):
    rows, width = query_rows.shape
    any_spec = pl.BlockSpec(memory_space=pl.ANY)
    vmem_spec = pl.BlockSpec(memory_space=pltpu.VMEM)
    vmem_limit = 16 * 1024 * 1024
    wide = jax.ShapeDtypeStruct((rows, width), BF16)
    small = jax.ShapeDtypeStruct((MODES, 512), F32)
    dma = pltpu.SemaphoreType.DMA
    whole = pltpu.VMEM((rows, width), BF16)
    outs = pl.pallas_call(
        kernel,
        out_shape=(whole, whole, whole, whole, pltpu.VMEM((CHUNKS, MODES, 128), BF16)),
        in_specs=[any_spec] * 6,
        out_specs=[vmem_spec] * 5,
        scratch_shapes=[whole] * 4
        + [
            pltpu.VMEM((2, MODES, 128), F32),
            pltpu.VMEM((64, 32, 128), BF16),
            pltpu.VMEM((CHUNKS, PER, 128), F32),
            pltpu.VMEM((CHUNKS, TOK, 128), BF16),
            pltpu.VMEM((CHUNKS, TOK, 256), BF16),
            pltpu.VMEM((CHUNKS, TOK, 256), F32),
            pltpu.VMEM((CHUNKS, PER, 128), F32),
            pltpu.VMEM((CHUNKS, 64, 128), BF16),
            pltpu.VMEM((PLANE, 64, 128), BF16),
            pltpu.VMEM((MODES, 128), F32),
            pltpu.VMEM((PLANE, MODES, 128), F32),
            pltpu.VMEM((32, 128), F32),
            pltpu.VMEM((32, 128), F32),
            pltpu.VMEM((MODES, 128), F32),
            pltpu.VMEM((MODES, 128), F32),
            pltpu.VMEM((MODES, 128), F32),
            pltpu.VMEM((PLANE, 32, 128), BF16),
            pltpu.VMEM((CHUNKS, 32, 128), BF16),
            pltpu.VMEM((MODES, 128), BF16),
            pltpu.VMEM((16, MODES, 128), BF16),
            pltpu.VMEM((MODES, 128), BF16),
            dma((4,)),
            dma((2,)),
            dma((6,)),
        ]
        + [dma(())] * 7
        + [pltpu.SemaphoreType.REGULAR],
        compiler_params=pltpu.CompilerParams(
            collective_id=0, has_side_effects=True, vmem_limit_bytes=vmem_limit
        ),
    )(
        *(
            pltpu.with_memory_space_constraint(x, pltpu.HBM)
            for x in (query_rows, key_rows, value_rows, grad_rows, residues.T, decay_rates.T)
        )
    )
    op, gq, gk, gv, gres, grate = pl.pallas_call(
        hand_over,
        out_shape=(wide, wide, wide, wide, small, small),
        in_specs=[vmem_spec] * 5,
        out_specs=[any_spec] * 6,
        scratch_shapes=[pltpu.VMEM((MODES, 512), F32)] * 2 + [dma((6,))],
        compiler_params=pltpu.CompilerParams(vmem_limit_bytes=vmem_limit),
    )(*outs)
    return op, gq, gk, gv, gres.T, grate.T


def solution(mesh):
    wide = P("ctx", "tensor")
    return jax.shard_map(
        per_device,
        mesh=mesh,
        in_specs=(wide, wide, wide, wide, P(), P()),
        out_specs=(wide, wide, wide, wide, P(), P()),
        check_vma=False,
    )
```

```python
import functools

import jax
import jax.numpy as jnp
from jax import lax
from jax.experimental import pallas as pl
from jax.experimental.pallas import tpu as pltpu
from jax.sharding import PartitionSpec as P

MESH = pl.DeviceIdType.MESH
F32 = jnp.float32
BF16 = jnp.bfloat16
EXACT = lax.Precision.HIGHEST

TOK = 128
CHUNKS = 8
PER = 8
GROUP = 16
MODES = 16
PLANE = 16
OWNERS = [4 * (k // 2) + k % 2 for k in range(CHUNKS)]
EARLY_FIRST = sorted(range(PLANE), key=lambda spot: spot // 4 + spot % 4)


def iota(shape, dim):
    return lax.broadcasted_iota(jnp.int32, shape, dim)


def dot(a, b, precision=None):
    return lax.dot_general(
        a, b, (((1,), (0,)), ((), ())), precision=precision, preferred_element_type=F32
    )


def dot_nt(a, b):
    return lax.dot_general(a, b, (((1,), (1,)), ((), ())), preferred_element_type=F32)


def kernel(
    q_hbm, k_hbm, v_hbm, g_hbm, res_hbm, rate_hbm,
    op_ref, gq_ref, gk_ref, gv_ref, grads_ref,
    q_v, k_v, v_v, g_v, par, wst, hrev, acoef, rhs, local, lagrev,
    send1, recv1, gsend, grecv, zsend, zrecv, wsend, wrecv, passing,
    send2, recv2, xsend, xrecv, ysend,
    in_sem, par_sem, send_sem,
    recv1_sem, recvg_sem, recvz_sem, recvw_sem, recv2_sem, recvx_sem, recvy_sem, ready_sem,
):
    ctx = lax.axis_index("ctx")
    tau = lax.axis_index("tensor")
    plane = ctx // PLANE
    me = ctx % PLANE
    z = plane * 4 + tau // 2
    core = tau % 2
    base = plane * PLANE
    first = plane == 0
    second = plane == 1
    x, y = me // 4, me % 4
    own_chunk = 2 * x + y
    owner = y < 2
    plain = jnp.logical_not(owner)
    first_owner = jnp.logical_and(first, owner)
    second_owner = jnp.logical_and(second, owner)

    def arrived(ref, count, sem):
        pltpu.make_async_copy(ref.at[pl.ds(0, count)], ref.at[pl.ds(0, count)], sem).wait()

    def arrived_from_owners(ref, sem):
        @pl.when(owner)
        def _():
            arrived(ref, CHUNKS - 1, sem)

        @pl.when(plain)
        def _():
            arrived(ref, CHUNKS, sem)

    def send(src, dst, kind, recv_sem, device):
        pltpu.make_async_remote_copy(
            src_ref=src,
            dst_ref=dst,
            send_sem=send_sem.at[kind],
            recv_sem=recv_sem,
            device_id=device,
            device_id_type=MESH,
        ).start()

    def signal(device):
        pl.semaphore_signal(barrier, inc=1, device_id=device, device_id_type=MESH)

    barrier = pltpu.get_barrier_semaphore()

    @pl.when(owner)
    def _():
        @pl.loop(1, PLANE)
        def _(i):
            signal({"ctx": base + (me + i) % PLANE})

        @pl.loop(1, 8)
        def _(i):
            signal({"tensor": (tau + i) % 8})

    @pl.when(first_owner)
    def _():
        @pl.loop(0, 8)
        def _(i):
            signal({"ctx": PLANE + me, "tensor": (tau + i) % 8})

    lanes = pl.ds(pl.multiple_of((tau // 2) * 128, 128), 128)
    par_copies = [
        pltpu.make_async_copy(res_hbm.at[:, lanes], par.at[0], par_sem.at[0]),
        pltpu.make_async_copy(rate_hbm.at[:, lanes], par.at[1], par_sem.at[1]),
    ]
    in_copies = [
        pltpu.make_async_copy(src, dst, in_sem.at[i])
        for i, (src, dst) in enumerate(((q_hbm, q_v), (k_hbm, k_v), (g_hbm, g_v), (v_hbm, v_v)))
    ]
    for copy in par_copies + in_copies:
        copy.start()

    for copy in par_copies:
        copy.wait()

    lane16 = iota((MODES, 128), 1)
    odd = (tau % 2) == 1

    def own_half(x):
        rolled = pltpu.roll(x, 64, 1)
        first = jnp.where(odd, rolled, x)
        return jnp.where(lane16 < 64, first, jnp.where(odd, x, rolled))

    res_t = own_half(par[0])
    rate_t = own_half(par[1])

    behind = (127 - lane16).astype(F32)
    ahead = (lane16 + 1).astype(F32)

    for k in range(CHUNKS):
        for i in range(PER):
            f = k * PER + i
            decay = jnp.exp(-rate_t[:, f : f + 1] * behind)
            wst[f, 0:16, :] = decay.astype(BF16)
            wst[f, 16:32, :] = (decay * behind).astype(BF16)

    for copy in in_copies:
        copy.wait()

    turn = (iota((TOK, TOK), 0) + iota((TOK, TOK), 1) == TOK - 1).astype(BF16)
    group_of = (iota((1, 256), 1) % 128) // GROUP

    for k in range(CHUNKS):
        cols = slice(128 * k, 128 * k + 128)
        rhs[k, :, 0:128] = (q_v[:, cols].astype(F32) * k_v[:, cols].astype(F32)).astype(BF16)
        dz = (g_v[:, cols].astype(F32) * v_v[:, cols].astype(F32)).astype(BF16)
        rhs[k, :, 128:256] = dot(turn, dz).astype(BF16)

    def end_states(chunks):
        for k in chunks:
            weights = wst[pl.ds(k * PER, PER)].reshape(PER * 32, TOK)
            ends = dot(weights, rhs[k])
            total = jnp.zeros((32, 256), F32)
            for i in range(PER):
                total = jnp.where(group_of == i, ends[32 * i : 32 * i + 32], total)
            toward = jnp.where(first, total[:, 0:128], total[:, 128:256])
            away = jnp.where(first, total[:, 128:256], total[:, 0:128])
            send1[k] = jnp.concatenate(
                [toward[0:16], away[0:16], toward[16:32], away[16:32]], axis=0
            ).astype(BF16)

    def send_ends(chunks):
        for k in chunks:
            peer = OWNERS[k]

            @pl.when(me != peer)
            def _():
                send(send1.at[k], recv1.at[place(me)], 0, recv1_sem, {"ctx": base + peer})

            @pl.when(me == peer)
            def _():
                recv1[place(me)] = send1[k]

    end_states(range(0, 4))

    @pl.when(plain)
    def _():
        pl.semaphore_wait(barrier, CHUNKS)

    @pl.when(first_owner)
    def _():
        pl.semaphore_wait(barrier, CHUNKS - 1 + 7)

    partner = {"ctx": (1 - plane) * PLANE + me}

    @pl.when(second_owner)
    def _():
        pl.semaphore_wait(barrier, CHUNKS - 1 + 7 + 8)

        @pl.loop(0, 8)
        def _(i):
            pl.semaphore_signal(
                ready_sem,
                inc=1,
                device_id={"ctx": me, "tensor": (tau + i) % 8},
                device_id_type=MESH,
            )

    def place(m):
        return jnp.where(first, m, PLANE - 1 - m)

    send_ends(range(0, 4))
    end_states(range(4, 8))
    send_ends(range(4, 8))

    row = iota((TOK, TOK), 0)
    lane = iota((TOK, TOK), 1)

    @pl.loop(0, CHUNKS, unroll=True)
    def _(k):
        u = rhs[k, :, 0:128]
        dz = rhs[k, :, 128:256]
        for i in range(PER):
            mine = jnp.where(group_of[:, 0:128] == i, dz, jnp.zeros_like(dz))
            pairs = dot_nt(mine, u)
            diag = pltpu.roll(pairs, 0, 1, stride=1, stride_axis=0)
            lagrev[k, i : i + 1, :] = jnp.sum(
                jnp.where(lane >= row, diag, 0.0), axis=0, keepdims=True
            )

    lag_all = lagrev[...].reshape(64, 128).astype(BF16)
    lag_all = jnp.concatenate([lag_all, lag_all], axis=0)
    lane_filter = iota((32, 128), 1)
    kind_filter = jnp.where(iota((32, 128), 0) < 16, lane_filter, lane_filter - 64)

    def add_filter(k, total):
        part = dot_nt(wst[pl.ds(k * PER, PER)].reshape(PER * 32, TOK), lag_all)
        for i in range(PER):
            total = jnp.where(kind_filter == k * PER + i, part[32 * i : 32 * i + 32], total)
        return total

    local_sums = lax.fori_loop(0, CHUNKS, add_filter, jnp.zeros((32, 128), F32), unroll=True)
    local_sums = local_sums[0:16] + local_sums[16:32]
    local_sums = jnp.where(lane16 < 64, local_sums, -res_t * local_sums)
    gsend[...] = local_sums.astype(BF16)
    for peer in OWNERS:

        @pl.when(me != peer)
        def _():
            send(gsend, grecv.at[me], 1, recvg_sem, {"ctx": base + peer})

    @pl.when(owner)
    def _():
        grecv[me] = gsend[...]

    for k in range(CHUNKS):
        powers = []
        for i in range(PER):
            f = k * PER + i
            rate = rate_t[:, f : f + 1]
            res = res_t[:, f : f + 1]
            decay = res * jnp.exp(-rate * behind)
            hrev[k, i : i + 1, :] = jnp.sum(decay, axis=0, keepdims=True)
            powers.append(res * jnp.exp(-rate * ahead))
        acoef[k] = jnp.concatenate(powers, axis=0).T.astype(BF16)

    @pl.loop(0, CHUNKS, unroll=True)
    def _(k):
        both = rhs[k]
        total = jnp.zeros((TOK, 256), F32)
        for i in range(PER):
            taps = pltpu.roll(
                jnp.broadcast_to(hrev[k, i : i + 1, :], (TOK, TOK)), 1, 1, stride=1, stride_axis=0
            )
            taps = jnp.where(lane <= row, taps, 0.0).astype(BF16)
            total = jnp.where(group_of == i, dot(taps, both), total)
        local[k] = total

    @pl.when(owner)
    def _():
        spread = (iota((128, 128), 0) == PER * own_chunk + iota((128, 128), 1) // GROUP).astype(F32)
        rate_spread = dot(rate_t, spread, EXACT)
        res_spread = dot(res_t, spread, EXACT)
        step = jnp.exp(-rate_spread * float(TOK))
        single = jnp.exp(-rate_spread)
        collect = (iota((128, 128), 1) % 64 == 8 * tau + iota((128, 128), 0) // GROUP).astype(BF16)
        zero = jnp.zeros((MODES, 128), F32)

        arrived(recv1, PLANE - 1, recv1_sem)

        states, one, two = [], zero, zero
        lag = float(TOK) * step
        for i in range(PLANE):
            states.append((one, two))
            two = step * two + (lag * one + recv1[i, 32:48, :].astype(F32))
            one = step * one + recv1[i, 0:16, :].astype(F32)

        @pl.when(first)
        def _():
            zsend[0:16] = one
            zsend[16:32] = two
            pl.semaphore_wait(ready_sem, 8)
            send(zsend, zrecv, 3, recvz_sem, partner)

        @pl.when(second)
        def _():
            wsend[...] = one
            send(wsend, wrecv, 3, recvw_sem, partner)

        sum_one, sum_two = zero, zero
        for i in range(PLANE):
            away_one, away_two = recv1[i, 16:32, :].astype(F32), recv1[i, 48:64, :].astype(F32)
            sum_one = sum_one + states[i][0] * away_one
            sum_two = sum_two + (states[i][1] * away_one + states[i][0] * (away_two + away_one))

        def collected(one_sum, two_sum):
            one_sum, two_sum = single * one_sum, -res_spread * single * two_sum
            one_high, two_high = one_sum.astype(BF16), two_sum.astype(BF16)
            parts = jnp.concatenate(
                [
                    one_high.astype(F32),
                    one_sum - one_high.astype(F32),
                    two_high.astype(F32),
                    two_sum - two_high.astype(F32),
                ],
                axis=0,
            ).astype(BF16)
            parts = dot(parts, collect)
            return jnp.where(lane16 < 64, parts[0:16] + parts[16:32], parts[32:48] + parts[48:64])

        def within_plane():
            arrived(grecv, PLANE - 1, recvg_sem)
            inside = jnp.where((lane16 % 64) // PER == own_chunk, jnp.sum(grecv[...].astype(F32), axis=0), 0.0)
            inside = pltpu.roll(inside, (128 + PER * (tau - own_chunk)) % 128, 1)
            return inside + collected(sum_one, sum_two)

        def send_along_z(grads):
            xsend[...] = grads.astype(BF16)
            for there in range(8):
                for other in (1, 0):
                    device = {"ctx": (there // 4) * PLANE + me, "tensor": (there % 4) * 2 + other}

                    @pl.when(jnp.logical_or(z != there, core != other))
                    def _():
                        send(xsend, xrecv.at[plane * 8 + tau], 4, recvx_sem, device)

            xrecv[plane * 8 + tau] = grads.astype(BF16)

        @pl.when(first)
        def _():
            send_along_z(within_plane())

        @pl.when(second)
        def _():
            grads = within_plane()
            pltpu.make_async_copy(zrecv, zrecv, recvz_sem).wait()
            other_one, other_two = zrecv[0:16], zrecv[16:32]
            passing[...] = other_one
            send_along_z(
                grads
                + collected(one * other_one, two * other_one + one * (other_two + other_one))
            )

        @pl.when(first)
        def _():
            pltpu.make_async_copy(wrecv, wrecv, recvw_sem).wait()
            passing[...] = wrecv[...]

        passed = passing[...]
        away = zero
        for i in reversed(range(PLANE)):
            toward, beside = states[i][0], away + passed
            send2[i] = jnp.concatenate(
                [jnp.where(first, toward, beside), jnp.where(first, beside, toward)], axis=0
            ).astype(BF16)
            away = step * away + recv1[i, 16:32, :].astype(F32)
            passed = step * passed
        for peer in EARLY_FIRST:

            @pl.when(me != peer)
            def _():
                send(send2.at[place(peer)], recv2.at[own_chunk], 2, recv2_sem, {"ctx": base + peer})

        recv2[own_chunk] = send2[place(me)]

        arrived(xrecv, 15, recvx_sem)
        total = jnp.sum(xrecv[...].astype(F32), axis=0).astype(BF16)
        ysend[...] = total
        for peer in EARLY_FIRST:

            @pl.when(me != peer)
            def _():
                send(ysend, grads_ref.at[own_chunk], 5, recvy_sem, {"ctx": base + peer})

        grads_ref[own_chunk] = total

    arrived_from_owners(recv2, recv2_sem)

    block_diagonal = (iota((PER, MODES, 256), 2) % 128) // GROUP == iota((PER, MODES, 256), 0)

    @pl.loop(0, CHUNKS, unroll=True)
    def _(k):
        cols = pl.ds(pl.multiple_of(k * 128, 128), 128)
        block = recv2[k]
        states = jnp.concatenate([block[0:16], block[16:32]], axis=1).astype(F32)
        states = jnp.where(block_diagonal, states[None], 0.0).reshape(PER * MODES, 256)
        total = local[k] + dot(acoef[k], states.astype(BF16))
        conv = total[:, 0:128].astype(BF16).astype(F32)
        back = dot(turn, total[:, 128:256].astype(BF16))
        op_ref[:, cols] = (v_v[:, cols].astype(F32) * conv).astype(BF16)
        gv_ref[:, cols] = (g_v[:, cols].astype(F32) * conv).astype(BF16)
        gq_ref[:, cols] = (k_v[:, cols].astype(F32) * back).astype(BF16)
        gk_ref[:, cols] = (q_v[:, cols].astype(F32) * back).astype(BF16)

    arrived_from_owners(send1, send_sem.at[0])
    arrived_from_owners(grecv, send_sem.at[1])

    @pl.when(first_owner)
    def _():
        pltpu.make_async_copy(zsend, zsend, send_sem.at[3]).wait()

    @pl.when(second_owner)
    def _():
        pltpu.make_async_copy(wsend, wsend, send_sem.at[3]).wait()

    @pl.when(owner)
    def _():
        arrived(send2, PLANE - 1, send_sem.at[2])
        arrived(xrecv, 15, send_sem.at[4])
        arrived(xrecv, PLANE - 1, send_sem.at[5])

    arrived_from_owners(grads_ref, recvy_sem)


def hand_over(
    op_v, gq_v, gk_v, gv_v, grads_v,
    op_out, gq_out, gk_out, gv_out, gres_out, grate_out,
    gres_v, grate_v, out_sem,
):
    held = (op_v, gq_v, gk_v, gv_v, gres_v, grate_v)
    results = (op_out, gq_out, gk_out, gv_out, gres_out, grate_out)
    out = [pltpu.make_async_copy(held[i], results[i], out_sem.at[i]) for i in range(6)]
    for copy in out[:4]:
        copy.start()

    lane = iota((MODES, 128), 1)
    rows = [
        grads_v[k].astype(F32) for k in range(CHUNKS)
    ]
    for bit in (4, 2, 1):
        clear = (lane // PER) % (2 * bit) < bit
        turned = list(rows)
        for k in range(CHUNKS):
            if k & bit:
                continue
            near, far = rows[k], rows[k + bit]
            turned[k] = jnp.where(clear, near, pltpu.roll(far, PER * bit, 1))
            turned[k + bit] = jnp.where(clear, pltpu.roll(near, 128 - PER * bit, 1), far)
        rows = turned
    for j in range(4):
        even, uneven = rows[2 * j], rows[2 * j + 1]
        gres_v[:, 128 * j : 128 * j + 128] = jnp.where(
            lane < 64, even, pltpu.roll(uneven, 64, 1)
        )
        grate_v[:, 128 * j : 128 * j + 128] = jnp.where(
            lane < 64, pltpu.roll(even, 64, 1), uneven
        )
    out[4].start()
    out[5].start()

    for copy in out:
        copy.wait()


def per_device(query_rows, key_rows, value_rows, grad_rows, residues, decay_rates):
    rows, width = query_rows.shape
    any_spec = pl.BlockSpec(memory_space=pl.ANY)
    vmem_spec = pl.BlockSpec(memory_space=pltpu.VMEM)
    vmem_limit = 16 * 1024 * 1024
    wide = jax.ShapeDtypeStruct((rows, width), BF16)
    small = jax.ShapeDtypeStruct((MODES, 512), F32)
    dma = pltpu.SemaphoreType.DMA
    whole = pltpu.VMEM((rows, width), BF16)
    outs = pl.pallas_call(
        kernel,
        out_shape=(whole, whole, whole, whole, pltpu.VMEM((CHUNKS, MODES, 128), BF16)),
        in_specs=[any_spec] * 6,
        out_specs=[vmem_spec] * 5,
        scratch_shapes=[whole] * 4
        + [
            pltpu.VMEM((2, MODES, 128), F32),
            pltpu.VMEM((64, 32, 128), BF16),
            pltpu.VMEM((CHUNKS, PER, 128), F32),
            pltpu.VMEM((CHUNKS, TOK, 128), BF16),
            pltpu.VMEM((CHUNKS, TOK, 256), BF16),
            pltpu.VMEM((CHUNKS, TOK, 256), F32),
            pltpu.VMEM((CHUNKS, PER, 128), F32),
            pltpu.VMEM((CHUNKS, 64, 128), BF16),
            pltpu.VMEM((PLANE, 64, 128), BF16),
            pltpu.VMEM((MODES, 128), BF16),
            pltpu.VMEM((PLANE, MODES, 128), BF16),
            pltpu.VMEM((32, 128), F32),
            pltpu.VMEM((32, 128), F32),
            pltpu.VMEM((MODES, 128), F32),
            pltpu.VMEM((MODES, 128), F32),
            pltpu.VMEM((MODES, 128), F32),
            pltpu.VMEM((PLANE, 32, 128), BF16),
            pltpu.VMEM((CHUNKS, 32, 128), BF16),
            pltpu.VMEM((MODES, 128), BF16),
            pltpu.VMEM((16, MODES, 128), BF16),
            pltpu.VMEM((MODES, 128), BF16),
            dma((4,)),
            dma((2,)),
            dma((6,)),
        ]
        + [dma(())] * 7
        + [pltpu.SemaphoreType.REGULAR],
        compiler_params=pltpu.CompilerParams(
            collective_id=0, has_side_effects=True, vmem_limit_bytes=vmem_limit
        ),
    )(
        *(
            pltpu.with_memory_space_constraint(x, pltpu.HBM)
            for x in (query_rows, key_rows, value_rows, grad_rows, residues.T, decay_rates.T)
        )
    )
    op, gq, gk, gv, gres, grate = pl.pallas_call(
        hand_over,
        out_shape=(wide, wide, wide, wide, small, small),
        in_specs=[vmem_spec] * 5,
        out_specs=[any_spec] * 6,
        scratch_shapes=[pltpu.VMEM((MODES, 512), F32)] * 2 + [dma((6,))],
        compiler_params=pltpu.CompilerParams(vmem_limit_bytes=vmem_limit),
    )(*outs)
    return op, gq, gk, gv, gres.T, grate.T


def solution(mesh):
    wide = P("ctx", "tensor")
    return jax.shard_map(
        per_device,
        mesh=mesh,
        in_specs=(wide, wide, wide, wide, P(), P()),
        out_specs=(wide, wide, wide, wide, P(), P()),
        check_vma=False,
    )
```

```python
import functools

import jax
import jax.numpy as jnp
from jax import lax
from jax.experimental import pallas as pl
from jax.experimental.pallas import tpu as pltpu
from jax.sharding import PartitionSpec as P

MESH = pl.DeviceIdType.MESH
F32 = jnp.float32
BF16 = jnp.bfloat16
EXACT = lax.Precision.HIGHEST

TOK = 128
CHUNKS = 8
PER = 8
GROUP = 16
MODES = 16
PLANE = 16
OWNERS = [4 * (k // 2) + k % 2 for k in range(CHUNKS)]
EARLY_FIRST = sorted(range(PLANE), key=lambda spot: spot // 4 + spot % 4)


def iota(shape, dim):
    return lax.broadcasted_iota(jnp.int32, shape, dim)


def dot(a, b, precision=None):
    return lax.dot_general(
        a, b, (((1,), (0,)), ((), ())), precision=precision, preferred_element_type=F32
    )


def dot_nt(a, b):
    return lax.dot_general(a, b, (((1,), (1,)), ((), ())), preferred_element_type=F32)


def kernel(
    q_hbm, k_hbm, v_hbm, g_hbm, res_hbm, rate_hbm,
    op_ref, gq_ref, gk_ref, gv_ref, grads_ref,
    q_v, k_v, v_v, g_v, par, wst, hrev, acoef, rhs, local, lagrev,
    send1, recv1, gsend, grecv, zsend, zrecv, wsend, wrecv, passing,
    send2, recv2, xsend, xrecv, ysend,
    in_sem, par_sem, send_sem,
    recv1_sem, recvg_sem, recvz_sem, recvw_sem, recv2_sem, recvx_sem, recvy_sem, ready_sem,
):
    ctx = lax.axis_index("ctx")
    tau = lax.axis_index("tensor")
    plane = ctx // PLANE
    me = ctx % PLANE
    z = plane * 4 + tau // 2
    core = tau % 2
    base = plane * PLANE
    first = plane == 0
    second = plane == 1
    x, y = me // 4, me % 4
    own_chunk = 2 * x + y
    owner = y < 2
    plain = jnp.logical_not(owner)
    first_owner = jnp.logical_and(first, owner)
    second_owner = jnp.logical_and(second, owner)

    def arrived(ref, count, sem):
        pltpu.make_async_copy(ref.at[pl.ds(0, count)], ref.at[pl.ds(0, count)], sem).wait()

    def arrived_from_owners(ref, sem):
        @pl.when(owner)
        def _():
            arrived(ref, CHUNKS - 1, sem)

        @pl.when(plain)
        def _():
            arrived(ref, CHUNKS, sem)

    def send(src, dst, kind, recv_sem, device):
        pltpu.make_async_remote_copy(
            src_ref=src,
            dst_ref=dst,
            send_sem=send_sem.at[kind],
            recv_sem=recv_sem,
            device_id=device,
            device_id_type=MESH,
        ).start()

    def signal(device):
        pl.semaphore_signal(barrier, inc=1, device_id=device, device_id_type=MESH)

    barrier = pltpu.get_barrier_semaphore()

    @pl.when(owner)
    def _():
        @pl.loop(1, PLANE)
        def _(i):
            signal({"ctx": base + (me + i) % PLANE})

        @pl.loop(1, 8)
        def _(i):
            signal({"tensor": (tau + i) % 8})

    @pl.when(first_owner)
    def _():
        @pl.loop(0, 8)
        def _(i):
            signal({"ctx": PLANE + me, "tensor": (tau + i) % 8})

    lanes = pl.ds(pl.multiple_of((tau // 2) * 128, 128), 128)
    par_copies = [
        pltpu.make_async_copy(res_hbm.at[:, lanes], par.at[0], par_sem.at[0]),
        pltpu.make_async_copy(rate_hbm.at[:, lanes], par.at[1], par_sem.at[1]),
    ]
    in_copies = [
        pltpu.make_async_copy(src, dst, in_sem.at[i])
        for i, (src, dst) in enumerate(((q_hbm, q_v), (k_hbm, k_v), (g_hbm, g_v), (v_hbm, v_v)))
    ]
    for copy in par_copies + in_copies:
        copy.start()

    for copy in par_copies:
        copy.wait()

    lane16 = iota((MODES, 128), 1)
    odd = (tau % 2) == 1

    def own_half(x):
        rolled = pltpu.roll(x, 64, 1)
        first = jnp.where(odd, rolled, x)
        return jnp.where(lane16 < 64, first, jnp.where(odd, x, rolled))

    res_t = own_half(par[0])
    rate_t = own_half(par[1])

    behind = (127 - lane16).astype(F32)
    ahead = (lane16 + 1).astype(F32)

    for k in range(CHUNKS):
        for i in range(PER):
            f = k * PER + i
            decay = jnp.exp(-rate_t[:, f : f + 1] * behind)
            wst[f, 0:16, :] = decay.astype(BF16)
            wst[f, 16:32, :] = (decay * behind).astype(BF16)

    for copy in in_copies:
        copy.wait()

    turn = (iota((TOK, TOK), 0) + iota((TOK, TOK), 1) == TOK - 1).astype(BF16)
    group_of = (iota((1, 256), 1) % 128) // GROUP

    for k in range(CHUNKS):
        cols = slice(128 * k, 128 * k + 128)
        rhs[k, :, 0:128] = (q_v[:, cols].astype(F32) * k_v[:, cols].astype(F32)).astype(BF16)
        dz = (g_v[:, cols].astype(F32) * v_v[:, cols].astype(F32)).astype(BF16)
        rhs[k, :, 128:256] = dot(turn, dz).astype(BF16)

    def end_states(chunks):
        for k in chunks:
            weights = wst[pl.ds(k * PER, PER)].reshape(PER * 32, TOK)
            ends = dot(weights, rhs[k])
            total = jnp.zeros((32, 256), F32)
            for i in range(PER):
                total = jnp.where(group_of == i, ends[32 * i : 32 * i + 32], total)
            toward = jnp.where(first, total[:, 0:128], total[:, 128:256])
            away = jnp.where(first, total[:, 128:256], total[:, 0:128])
            send1[k] = jnp.concatenate(
                [toward[0:16], away[0:16], toward[16:32], away[16:32]], axis=0
            ).astype(BF16)

    def send_ends(chunks):
        for k in chunks:
            peer = OWNERS[k]

            @pl.when(me != peer)
            def _():
                send(send1.at[k], recv1.at[place(me)], 0, recv1_sem, {"ctx": base + peer})

            @pl.when(me == peer)
            def _():
                recv1[place(me)] = send1[k]

    end_states(range(0, 4))

    @pl.when(plain)
    def _():
        pl.semaphore_wait(barrier, CHUNKS)

    @pl.when(first_owner)
    def _():
        pl.semaphore_wait(barrier, CHUNKS - 1 + 7)

    partner = {"ctx": (1 - plane) * PLANE + me}

    @pl.when(second_owner)
    def _():
        pl.semaphore_wait(barrier, CHUNKS - 1 + 7 + 8)

        @pl.loop(0, 8)
        def _(i):
            pl.semaphore_signal(
                ready_sem,
                inc=1,
                device_id={"ctx": me, "tensor": (tau + i) % 8},
                device_id_type=MESH,
            )

    def place(m):
        return jnp.where(first, m, PLANE - 1 - m)

    send_ends(range(0, 4))
    end_states(range(4, 8))
    send_ends(range(4, 8))

    row = iota((TOK, TOK), 0)
    lane = iota((TOK, TOK), 1)

    @pl.loop(0, CHUNKS, unroll=True)
    def _(k):
        u = rhs[k, :, 0:128]
        dz = rhs[k, :, 128:256]
        for i in range(PER):
            mine = jnp.where(group_of[:, 0:128] == i, dz, jnp.zeros_like(dz))
            pairs = dot_nt(mine, u)
            diag = pltpu.roll(pairs, 0, 1, stride=1, stride_axis=0)
            lagrev[k, i : i + 1, :] = jnp.sum(
                jnp.where(lane >= row, diag, 0.0), axis=0, keepdims=True
            )

    lag_all = lagrev[...].reshape(64, 128).astype(BF16)
    lag_all = jnp.concatenate([lag_all, lag_all], axis=0)
    lane_filter = iota((32, 128), 1)
    kind_filter = jnp.where(iota((32, 128), 0) < 16, lane_filter, lane_filter - 64)

    def add_filter(k, total):
        part = dot_nt(wst[pl.ds(k * PER, PER)].reshape(PER * 32, TOK), lag_all)
        for i in range(PER):
            total = jnp.where(kind_filter == k * PER + i, part[32 * i : 32 * i + 32], total)
        return total

    local_sums = lax.fori_loop(0, CHUNKS, add_filter, jnp.zeros((32, 128), F32), unroll=True)
    local_sums = local_sums[0:16] + local_sums[16:32]
    local_sums = jnp.where(lane16 < 64, local_sums, -res_t * local_sums)
    gsend[...] = local_sums.astype(BF16)
    for peer in OWNERS:

        @pl.when(me != peer)
        def _():
            send(gsend, grecv.at[me], 1, recvg_sem, {"ctx": base + peer})

    @pl.when(owner)
    def _():
        grecv[me] = gsend[...]

    for k in range(CHUNKS):
        powers = []
        for i in range(PER):
            f = k * PER + i
            rate = rate_t[:, f : f + 1]
            res = res_t[:, f : f + 1]
            decay = res * jnp.exp(-rate * behind)
            hrev[k, i : i + 1, :] = jnp.sum(decay, axis=0, keepdims=True)
            powers.append(res * jnp.exp(-rate * ahead))
        acoef[k] = jnp.concatenate(powers, axis=0).T.astype(BF16)

    @pl.loop(0, CHUNKS, unroll=True)
    def _(k):
        both = rhs[k]
        total = jnp.zeros((TOK, 256), F32)
        for i in range(PER):
            taps = pltpu.roll(
                jnp.broadcast_to(hrev[k, i : i + 1, :], (TOK, TOK)), 1, 1, stride=1, stride_axis=0
            )
            taps = jnp.where(lane <= row, taps, 0.0).astype(BF16)
            total = jnp.where(group_of == i, dot(taps, both), total)
        local[k] = total

    @pl.when(owner)
    def _():
        spread = (iota((128, 128), 0) == PER * own_chunk + iota((128, 128), 1) // GROUP).astype(F32)
        rate_spread = dot(rate_t, spread, EXACT)
        res_spread = dot(res_t, spread, EXACT)
        step = jnp.exp(-rate_spread * float(TOK))
        single = jnp.exp(-rate_spread)
        collect = (iota((128, 128), 1) % 64 == 8 * tau + iota((128, 128), 0) // GROUP).astype(BF16)
        zero = jnp.zeros((MODES, 128), F32)

        arrived(recv1, PLANE - 1, recv1_sem)

        states, one, two = [], zero, zero
        lag = float(TOK) * step
        for i in range(PLANE):
            states.append((one, two))
            two = step * two + (lag * one + recv1[i, 32:48, :].astype(F32))
            one = step * one + recv1[i, 0:16, :].astype(F32)

        @pl.when(first)
        def _():
            zsend[0:16] = one.astype(BF16)
            zsend[16:32] = two.astype(BF16)
            pl.semaphore_wait(ready_sem, 8)
            send(zsend, zrecv, 3, recvz_sem, partner)

        @pl.when(second)
        def _():
            wsend[...] = one
            send(wsend, wrecv, 3, recvw_sem, partner)

        sum_one, sum_two = zero, zero
        for i in range(PLANE):
            away_one, away_two = recv1[i, 16:32, :].astype(F32), recv1[i, 48:64, :].astype(F32)
            sum_one = sum_one + states[i][0] * away_one
            sum_two = sum_two + (states[i][1] * away_one + states[i][0] * (away_two + away_one))

        def collected(one_sum, two_sum):
            one_sum, two_sum = single * one_sum, -res_spread * single * two_sum
            parts = dot(jnp.concatenate([one_sum, two_sum], axis=0).astype(BF16), collect)
            return jnp.where(lane16 < 64, parts[0:16], parts[16:32])

        def within_plane():
            arrived(grecv, PLANE - 1, recvg_sem)
            inside = jnp.where((lane16 % 64) // PER == own_chunk, jnp.sum(grecv[...].astype(F32), axis=0), 0.0)
            inside = pltpu.roll(inside, (128 + PER * (tau - own_chunk)) % 128, 1)
            return inside + collected(sum_one, sum_two)

        def send_along_z(grads):
            xsend[...] = grads.astype(BF16)
            for there in range(8):
                for other in (1, 0):
                    device = {"ctx": (there // 4) * PLANE + me, "tensor": (there % 4) * 2 + other}

                    @pl.when(jnp.logical_or(z != there, core != other))
                    def _():
                        send(xsend, xrecv.at[plane * 8 + tau], 4, recvx_sem, device)

            xrecv[plane * 8 + tau] = grads.astype(BF16)

        @pl.when(first)
        def _():
            send_along_z(within_plane())

        @pl.when(second)
        def _():
            grads = within_plane()
            pltpu.make_async_copy(zrecv, zrecv, recvz_sem).wait()
            other_one, other_two = zrecv[0:16].astype(F32), zrecv[16:32].astype(F32)
            passing[...] = other_one
            send_along_z(
                grads
                + collected(one * other_one, two * other_one + one * (other_two + other_one))
            )

        @pl.when(first)
        def _():
            pltpu.make_async_copy(wrecv, wrecv, recvw_sem).wait()
            passing[...] = wrecv[...]

        passed = passing[...]
        away = zero
        for i in reversed(range(PLANE)):
            toward, beside = states[i][0], away + passed
            send2[i] = jnp.concatenate(
                [jnp.where(first, toward, beside), jnp.where(first, beside, toward)], axis=0
            ).astype(BF16)
            away = step * away + recv1[i, 16:32, :].astype(F32)
            passed = step * passed
        for peer in EARLY_FIRST:

            @pl.when(me != peer)
            def _():
                send(send2.at[place(peer)], recv2.at[own_chunk], 2, recv2_sem, {"ctx": base + peer})

        recv2[own_chunk] = send2[place(me)]

        arrived(xrecv, 15, recvx_sem)
        total = jnp.sum(xrecv[...].astype(F32), axis=0).astype(BF16)
        ysend[...] = total
        for peer in EARLY_FIRST:

            @pl.when(me != peer)
            def _():
                send(ysend, grads_ref.at[own_chunk], 5, recvy_sem, {"ctx": base + peer})

        grads_ref[own_chunk] = total

    arrived_from_owners(recv2, recv2_sem)

    block_diagonal = (iota((PER, MODES, 256), 2) % 128) // GROUP == iota((PER, MODES, 256), 0)

    @pl.loop(0, CHUNKS, unroll=True)
    def _(k):
        cols = pl.ds(pl.multiple_of(k * 128, 128), 128)
        block = recv2[k]
        states = jnp.concatenate([block[0:16], block[16:32]], axis=1).astype(F32)
        states = jnp.where(block_diagonal, states[None], 0.0).reshape(PER * MODES, 256)
        total = local[k] + dot(acoef[k], states.astype(BF16))
        conv = total[:, 0:128].astype(BF16).astype(F32)
        back = dot(turn, total[:, 128:256].astype(BF16))
        op_ref[:, cols] = (v_v[:, cols].astype(F32) * conv).astype(BF16)
        gv_ref[:, cols] = (g_v[:, cols].astype(F32) * conv).astype(BF16)
        gq_ref[:, cols] = (k_v[:, cols].astype(F32) * back).astype(BF16)
        gk_ref[:, cols] = (q_v[:, cols].astype(F32) * back).astype(BF16)

    arrived_from_owners(send1, send_sem.at[0])
    arrived_from_owners(grecv, send_sem.at[1])

    @pl.when(first_owner)
    def _():
        pltpu.make_async_copy(zsend, zsend, send_sem.at[3]).wait()

    @pl.when(second_owner)
    def _():
        pltpu.make_async_copy(wsend, wsend, send_sem.at[3]).wait()

    @pl.when(owner)
    def _():
        arrived(send2, PLANE - 1, send_sem.at[2])
        arrived(xrecv, 15, send_sem.at[4])
        arrived(xrecv, PLANE - 1, send_sem.at[5])

    arrived_from_owners(grads_ref, recvy_sem)


def hand_over(
    op_v, gq_v, gk_v, gv_v, grads_v,
    op_out, gq_out, gk_out, gv_out, gres_out, grate_out,
    gres_v, grate_v, out_sem,
):
    held = (op_v, gq_v, gk_v, gv_v, gres_v, grate_v)
    results = (op_out, gq_out, gk_out, gv_out, gres_out, grate_out)
    out = [pltpu.make_async_copy(held[i], results[i], out_sem.at[i]) for i in range(6)]
    for copy in out[:4]:
        copy.start()

    lane = iota((MODES, 128), 1)
    rows = [
        grads_v[k].astype(F32) for k in range(CHUNKS)
    ]
    for bit in (4, 2, 1):
        clear = (lane // PER) % (2 * bit) < bit
        turned = list(rows)
        for k in range(CHUNKS):
            if k & bit:
                continue
            near, far = rows[k], rows[k + bit]
            turned[k] = jnp.where(clear, near, pltpu.roll(far, PER * bit, 1))
            turned[k + bit] = jnp.where(clear, pltpu.roll(near, 128 - PER * bit, 1), far)
        rows = turned
    for j in range(4):
        even, uneven = rows[2 * j], rows[2 * j + 1]
        gres_v[:, 128 * j : 128 * j + 128] = jnp.where(
            lane < 64, even, pltpu.roll(uneven, 64, 1)
        )
        grate_v[:, 128 * j : 128 * j + 128] = jnp.where(
            lane < 64, pltpu.roll(even, 64, 1), uneven
        )
    out[4].start()
    out[5].start()

    for copy in out:
        copy.wait()


def per_device(query_rows, key_rows, value_rows, grad_rows, residues, decay_rates):
    rows, width = query_rows.shape
    any_spec = pl.BlockSpec(memory_space=pl.ANY)
    vmem_spec = pl.BlockSpec(memory_space=pltpu.VMEM)
    vmem_limit = 16 * 1024 * 1024
    wide = jax.ShapeDtypeStruct((rows, width), BF16)
    small = jax.ShapeDtypeStruct((MODES, 512), F32)
    dma = pltpu.SemaphoreType.DMA
    whole = pltpu.VMEM((rows, width), BF16)
    outs = pl.pallas_call(
        kernel,
        out_shape=(whole, whole, whole, whole, pltpu.VMEM((CHUNKS, MODES, 128), BF16)),
        in_specs=[any_spec] * 6,
        out_specs=[vmem_spec] * 5,
        scratch_shapes=[whole] * 4
        + [
            pltpu.VMEM((2, MODES, 128), F32),
            pltpu.VMEM((64, 32, 128), BF16),
            pltpu.VMEM((CHUNKS, PER, 128), F32),
            pltpu.VMEM((CHUNKS, TOK, 128), BF16),
            pltpu.VMEM((CHUNKS, TOK, 256), BF16),
            pltpu.VMEM((CHUNKS, TOK, 256), F32),
            pltpu.VMEM((CHUNKS, PER, 128), F32),
            pltpu.VMEM((CHUNKS, 64, 128), BF16),
            pltpu.VMEM((PLANE, 64, 128), BF16),
            pltpu.VMEM((MODES, 128), BF16),
            pltpu.VMEM((PLANE, MODES, 128), BF16),
            pltpu.VMEM((32, 128), BF16),
            pltpu.VMEM((32, 128), BF16),
            pltpu.VMEM((MODES, 128), F32),
            pltpu.VMEM((MODES, 128), F32),
            pltpu.VMEM((MODES, 128), F32),
            pltpu.VMEM((PLANE, 32, 128), BF16),
            pltpu.VMEM((CHUNKS, 32, 128), BF16),
            pltpu.VMEM((MODES, 128), BF16),
            pltpu.VMEM((16, MODES, 128), BF16),
            pltpu.VMEM((MODES, 128), BF16),
            dma((4,)),
            dma((2,)),
            dma((6,)),
        ]
        + [dma(())] * 7
        + [pltpu.SemaphoreType.REGULAR],
        compiler_params=pltpu.CompilerParams(
            collective_id=0, has_side_effects=True, vmem_limit_bytes=vmem_limit
        ),
    )(
        *(
            pltpu.with_memory_space_constraint(x, pltpu.HBM)
            for x in (query_rows, key_rows, value_rows, grad_rows, residues.T, decay_rates.T)
        )
    )
    op, gq, gk, gv, gres, grate = pl.pallas_call(
        hand_over,
        out_shape=(wide, wide, wide, wide, small, small),
        in_specs=[vmem_spec] * 5,
        out_specs=[any_spec] * 6,
        scratch_shapes=[pltpu.VMEM((MODES, 512), F32)] * 2 + [dma((6,))],
        compiler_params=pltpu.CompilerParams(vmem_limit_bytes=vmem_limit),
    )(*outs)
    return op, gq, gk, gv, gres.T, grate.T


def solution(mesh):
    wide = P("ctx", "tensor")
    return jax.shard_map(
        per_device,
        mesh=mesh,
        in_specs=(wide, wide, wide, wide, P(), P()),
        out_specs=(wide, wide, wide, wide, P(), P()),
        check_vma=False,
    )
```

```python
import functools

import jax
import jax.numpy as jnp
from jax import lax
from jax.experimental import pallas as pl
from jax.experimental.pallas import tpu as pltpu
from jax.sharding import PartitionSpec as P

MESH = pl.DeviceIdType.MESH
F32 = jnp.float32
BF16 = jnp.bfloat16
EXACT = lax.Precision.HIGHEST

TOK = 128
CHUNKS = 8
PER = 8
GROUP = 16
MODES = 16
PLANE = 16
OWNERS = [4 * (k // 2) + k % 2 for k in range(CHUNKS)]
EARLY_FIRST = sorted(range(PLANE), key=lambda spot: spot // 4 + spot % 4)


def iota(shape, dim):
    return lax.broadcasted_iota(jnp.int32, shape, dim)


def dot(a, b, precision=None):
    return lax.dot_general(
        a, b, (((1,), (0,)), ((), ())), precision=precision, preferred_element_type=F32
    )


def dot_nt(a, b):
    return lax.dot_general(a, b, (((1,), (1,)), ((), ())), preferred_element_type=F32)


def kernel(
    q_hbm, k_hbm, v_hbm, g_hbm, res_hbm, rate_hbm,
    op_ref, gq_ref, gk_ref, gv_ref, grads_ref,
    q_v, k_v, v_v, g_v, par, wst, hrev, acoef, rhs, local, lagrev,
    send1, recv1, gsend, grecv, zsend, zrecv, wsend, wrecv, passing,
    send2, recv2, xsend, xrecv, ysend,
    in_sem, par_sem, send_sem,
    recv1_sem, recvg_sem, recvz_sem, recvw_sem, recv2_sem, recvx_sem, recvy_sem, ready_sem,
):
    ctx = lax.axis_index("ctx")
    tau = lax.axis_index("tensor")
    plane = ctx // PLANE
    me = ctx % PLANE
    z = plane * 4 + tau // 2
    core = tau % 2
    base = plane * PLANE
    first = plane == 0
    second = plane == 1
    x, y = me // 4, me % 4
    own_chunk = 2 * x + y
    owner = y < 2
    plain = jnp.logical_not(owner)
    first_owner = jnp.logical_and(first, owner)
    second_owner = jnp.logical_and(second, owner)

    def arrived(ref, count, sem):
        pltpu.make_async_copy(ref.at[pl.ds(0, count)], ref.at[pl.ds(0, count)], sem).wait()

    def arrived_from_owners(ref, sem):
        @pl.when(owner)
        def _():
            arrived(ref, CHUNKS - 1, sem)

        @pl.when(plain)
        def _():
            arrived(ref, CHUNKS, sem)

    def send(src, dst, kind, recv_sem, device):
        pltpu.make_async_remote_copy(
            src_ref=src,
            dst_ref=dst,
            send_sem=send_sem.at[kind],
            recv_sem=recv_sem,
            device_id=device,
            device_id_type=MESH,
        ).start()

    def signal(device):
        pl.semaphore_signal(barrier, inc=1, device_id=device, device_id_type=MESH)

    barrier = pltpu.get_barrier_semaphore()

    @pl.when(owner)
    def _():
        @pl.loop(1, PLANE)
        def _(i):
            signal({"ctx": base + (me + i) % PLANE})

        @pl.loop(1, 8)
        def _(i):
            signal({"tensor": (tau + i) % 8})

    @pl.when(first_owner)
    def _():
        @pl.loop(0, 8)
        def _(i):
            signal({"ctx": PLANE + me, "tensor": (tau + i) % 8})

    lanes = pl.ds(pl.multiple_of((tau // 2) * 128, 128), 128)
    par_copies = [
        pltpu.make_async_copy(res_hbm.at[:, lanes], par.at[0], par_sem.at[0]),
        pltpu.make_async_copy(rate_hbm.at[:, lanes], par.at[1], par_sem.at[1]),
    ]
    in_copies = [
        pltpu.make_async_copy(src, dst, in_sem.at[i])
        for i, (src, dst) in enumerate(((q_hbm, q_v), (k_hbm, k_v), (g_hbm, g_v), (v_hbm, v_v)))
    ]
    for copy in par_copies + in_copies:
        copy.start()

    for copy in par_copies:
        copy.wait()

    lane16 = iota((MODES, 128), 1)
    odd = (tau % 2) == 1

    def own_half(x):
        rolled = pltpu.roll(x, 64, 1)
        first = jnp.where(odd, rolled, x)
        return jnp.where(lane16 < 64, first, jnp.where(odd, x, rolled))

    res_t = own_half(par[0])
    rate_t = own_half(par[1])

    behind = (127 - lane16).astype(F32)
    ahead = (lane16 + 1).astype(F32)

    for k in range(CHUNKS):
        for i in range(PER):
            f = k * PER + i
            decay = jnp.exp(-rate_t[:, f : f + 1] * behind)
            wst[f, 0:16, :] = decay.astype(BF16)
            wst[f, 16:32, :] = (decay * behind).astype(BF16)

    for copy in in_copies:
        copy.wait()

    turn = (iota((TOK, TOK), 0) + iota((TOK, TOK), 1) == TOK - 1).astype(BF16)
    group_of = (iota((1, 256), 1) % 128) // GROUP

    for k in range(CHUNKS):
        cols = slice(128 * k, 128 * k + 128)
        rhs[k, :, 0:128] = (q_v[:, cols].astype(F32) * k_v[:, cols].astype(F32)).astype(BF16)
        dz = (g_v[:, cols].astype(F32) * v_v[:, cols].astype(F32)).astype(BF16)
        rhs[k, :, 128:256] = dot(turn, dz).astype(BF16)

    def end_states(chunks):
        for k in chunks:
            weights = wst[pl.ds(k * PER, PER)].reshape(PER * 32, TOK)
            ends = dot(weights, rhs[k])
            total = jnp.zeros((32, 256), F32)
            for i in range(PER):
                total = jnp.where(group_of == i, ends[32 * i : 32 * i + 32], total)
            toward = jnp.where(first, total[:, 0:128], total[:, 128:256])
            away = jnp.where(first, total[:, 128:256], total[:, 0:128])
            send1[k] = jnp.concatenate(
                [toward[0:16], away[0:16], toward[16:32], away[16:32]], axis=0
            ).astype(BF16)

    def send_ends(chunks):
        for k in chunks:
            peer = OWNERS[k]

            @pl.when(me != peer)
            def _():
                send(send1.at[k], recv1.at[place(me)], 0, recv1_sem, {"ctx": base + peer})

            @pl.when(me == peer)
            def _():
                recv1[place(me)] = send1[k]

    end_states(range(0, 4))

    @pl.when(plain)
    def _():
        pl.semaphore_wait(barrier, CHUNKS)

    @pl.when(first_owner)
    def _():
        pl.semaphore_wait(barrier, CHUNKS - 1 + 7)

    partner = {"ctx": (1 - plane) * PLANE + me}

    @pl.when(second_owner)
    def _():
        pl.semaphore_wait(barrier, CHUNKS - 1 + 7 + 8)

        @pl.loop(0, 8)
        def _(i):
            pl.semaphore_signal(
                ready_sem,
                inc=1,
                device_id={"ctx": me, "tensor": (tau + i) % 8},
                device_id_type=MESH,
            )

    def place(m):
        return jnp.where(first, m, PLANE - 1 - m)

    send_ends(range(0, 4))
    end_states(range(4, 8))
    send_ends(range(4, 8))

    row = iota((TOK, TOK), 0)
    lane = iota((TOK, TOK), 1)

    @pl.loop(0, CHUNKS, unroll=True)
    def _(k):
        u = rhs[k, :, 0:128]
        dz = rhs[k, :, 128:256]
        for i in range(PER):
            mine = jnp.where(group_of[:, 0:128] == i, dz, jnp.zeros_like(dz))
            pairs = dot_nt(mine, u)
            diag = pltpu.roll(pairs, 0, 1, stride=1, stride_axis=0)
            lagrev[k, i : i + 1, :] = jnp.sum(
                jnp.where(lane >= row, diag, 0.0), axis=0, keepdims=True
            )

    lag_all = lagrev[...].reshape(64, 128).astype(BF16)
    lag_all = jnp.concatenate([lag_all, lag_all], axis=0)
    lane_filter = iota((32, 128), 1)
    kind_filter = jnp.where(iota((32, 128), 0) < 16, lane_filter, lane_filter - 64)

    def add_filter(k, total):
        part = dot_nt(wst[pl.ds(k * PER, PER)].reshape(PER * 32, TOK), lag_all)
        for i in range(PER):
            total = jnp.where(kind_filter == k * PER + i, part[32 * i : 32 * i + 32], total)
        return total

    local_sums = lax.fori_loop(0, CHUNKS, add_filter, jnp.zeros((32, 128), F32), unroll=True)
    local_sums = local_sums[0:16] + local_sums[16:32]
    local_sums = jnp.where(lane16 < 64, local_sums, -res_t * local_sums)
    gsend[...] = local_sums.astype(BF16)
    for peer in OWNERS:

        @pl.when(me != peer)
        def _():
            send(gsend, grecv.at[me], 1, recvg_sem, {"ctx": base + peer})

    @pl.when(owner)
    def _():
        grecv[me] = gsend[...]

    for k in range(CHUNKS):
        powers = []
        for i in range(PER):
            f = k * PER + i
            rate = rate_t[:, f : f + 1]
            res = res_t[:, f : f + 1]
            decay = res * jnp.exp(-rate * behind)
            hrev[k, i : i + 1, :] = jnp.sum(decay, axis=0, keepdims=True)
            powers.append(res * jnp.exp(-rate * ahead))
        acoef[k] = jnp.concatenate(powers, axis=0).T.astype(BF16)

    @pl.loop(0, CHUNKS, unroll=True)
    def _(k):
        both = rhs[k]
        total = jnp.zeros((TOK, 256), F32)
        for i in range(PER):
            taps = pltpu.roll(
                jnp.broadcast_to(hrev[k, i : i + 1, :], (TOK, TOK)), 1, 1, stride=1, stride_axis=0
            )
            taps = jnp.where(lane <= row, taps, 0.0).astype(BF16)
            total = jnp.where(group_of == i, dot(taps, both), total)
        local[k] = total

    @pl.when(owner)
    def _():
        spread = (iota((128, 128), 0) == PER * own_chunk + iota((128, 128), 1) // GROUP).astype(F32)
        rate_spread = dot(rate_t, spread, EXACT)
        res_spread = dot(res_t, spread, EXACT)
        step = jnp.exp(-rate_spread * float(TOK))
        single = jnp.exp(-rate_spread)
        collect = (iota((128, 128), 1) % 64 == 8 * tau + iota((128, 128), 0) // GROUP).astype(BF16)
        zero = jnp.zeros((MODES, 128), F32)

        arrived(recv1, PLANE - 1, recv1_sem)

        states, one, two = [], zero, zero
        lag = float(TOK) * step
        for i in range(PLANE):
            states.append((one, two))
            two = step * two + (lag * one + recv1[i, 32:48, :].astype(F32))
            one = step * one + recv1[i, 0:16, :].astype(F32)

        @pl.when(first)
        def _():
            zsend[0:16] = one
            zsend[16:32] = two
            pl.semaphore_wait(ready_sem, 8)
            send(zsend, zrecv, 3, recvz_sem, partner)

        @pl.when(second)
        def _():
            wsend[...] = one
            send(wsend, wrecv, 3, recvw_sem, partner)

        sum_one, sum_two = zero, zero
        for i in range(PLANE):
            away_one, away_two = recv1[i, 16:32, :].astype(F32), recv1[i, 48:64, :].astype(F32)
            sum_one = sum_one + states[i][0] * away_one
            sum_two = sum_two + (states[i][1] * away_one + states[i][0] * (away_two + away_one))

        def collected(one_sum, two_sum):
            one_sum, two_sum = single * one_sum, -res_spread * single * two_sum
            parts = dot(jnp.concatenate([one_sum, two_sum], axis=0).astype(BF16), collect)
            return jnp.where(lane16 < 64, parts[0:16], parts[16:32])

        def within_plane():
            arrived(grecv, PLANE - 1, recvg_sem)
            inside = jnp.where((lane16 % 64) // PER == own_chunk, jnp.sum(grecv[...].astype(F32), axis=0), 0.0)
            inside = pltpu.roll(inside, (128 + PER * (tau - own_chunk)) % 128, 1)
            return inside + collected(sum_one, sum_two)

        def send_along_z(grads):
            xsend[...] = grads.astype(BF16)
            for there in range(8):
                for other in (1, 0):
                    device = {"ctx": (there // 4) * PLANE + me, "tensor": (there % 4) * 2 + other}

                    @pl.when(jnp.logical_or(z != there, core != other))
                    def _():
                        send(xsend, xrecv.at[plane * 8 + tau], 4, recvx_sem, device)

            xrecv[plane * 8 + tau] = grads.astype(BF16)

        @pl.when(first)
        def _():
            send_along_z(within_plane())

        @pl.when(second)
        def _():
            grads = within_plane()
            pltpu.make_async_copy(zrecv, zrecv, recvz_sem).wait()
            other_one, other_two = zrecv[0:16], zrecv[16:32]
            passing[...] = other_one
            send_along_z(
                grads
                + collected(one * other_one, two * other_one + one * (other_two + other_one))
            )

        @pl.when(first)
        def _():
            pltpu.make_async_copy(wrecv, wrecv, recvw_sem).wait()
            passing[...] = wrecv[...]

        passed = passing[...]
        away = zero
        for i in reversed(range(PLANE)):
            toward, beside = states[i][0], away + passed
            send2[i] = jnp.concatenate(
                [jnp.where(first, toward, beside), jnp.where(first, beside, toward)], axis=0
            ).astype(BF16)
            away = step * away + recv1[i, 16:32, :].astype(F32)
            passed = step * passed
        for peer in EARLY_FIRST:

            @pl.when(me != peer)
            def _():
                send(send2.at[place(peer)], recv2.at[own_chunk], 2, recv2_sem, {"ctx": base + peer})

        recv2[own_chunk] = send2[place(me)]

        arrived(xrecv, 15, recvx_sem)
        total = jnp.sum(xrecv[...].astype(F32), axis=0).astype(BF16)
        ysend[...] = total
        for peer in EARLY_FIRST:

            @pl.when(me != peer)
            def _():
                send(ysend, grads_ref.at[own_chunk], 5, recvy_sem, {"ctx": base + peer})

        grads_ref[own_chunk] = total

    arrived_from_owners(recv2, recv2_sem)

    block_diagonal = (iota((PER, MODES, 256), 2) % 128) // GROUP == iota((PER, MODES, 256), 0)

    @pl.loop(0, CHUNKS, unroll=True)
    def _(k):
        cols = pl.ds(pl.multiple_of(k * 128, 128), 128)
        block = recv2[k]
        states = jnp.concatenate([block[0:16], block[16:32]], axis=1).astype(F32)
        states = jnp.where(block_diagonal, states[None], 0.0).reshape(PER * MODES, 256)
        total = local[k] + dot(acoef[k], states.astype(BF16))
        conv = total[:, 0:128].astype(BF16).astype(F32)
        back = dot(turn, total[:, 128:256].astype(BF16))
        op_ref[:, cols] = (v_v[:, cols].astype(F32) * conv).astype(BF16)
        gv_ref[:, cols] = (g_v[:, cols].astype(F32) * conv).astype(BF16)
        gq_ref[:, cols] = (k_v[:, cols].astype(F32) * back).astype(BF16)
        gk_ref[:, cols] = (q_v[:, cols].astype(F32) * back).astype(BF16)

    arrived_from_owners(send1, send_sem.at[0])
    arrived_from_owners(grecv, send_sem.at[1])

    @pl.when(first_owner)
    def _():
        pltpu.make_async_copy(zsend, zsend, send_sem.at[3]).wait()

    @pl.when(second_owner)
    def _():
        pltpu.make_async_copy(wsend, wsend, send_sem.at[3]).wait()

    @pl.when(owner)
    def _():
        arrived(send2, PLANE - 1, send_sem.at[2])
        arrived(xrecv, 15, send_sem.at[4])
        arrived(xrecv, PLANE - 1, send_sem.at[5])

    arrived_from_owners(grads_ref, recvy_sem)


def hand_over(
    op_v, gq_v, gk_v, gv_v, grads_v,
    op_out, gq_out, gk_out, gv_out, gres_out, grate_out,
    gres_v, grate_v, out_sem,
):
    held = (op_v, gq_v, gk_v, gv_v, gres_v, grate_v)
    results = (op_out, gq_out, gk_out, gv_out, gres_out, grate_out)
    out = [pltpu.make_async_copy(held[i], results[i], out_sem.at[i]) for i in range(6)]
    for copy in out[:4]:
        copy.start()

    lane = iota((MODES, 128), 1)
    rows = [
        grads_v[k].astype(F32) for k in range(CHUNKS)
    ]
    for bit in (4, 2, 1):
        clear = (lane // PER) % (2 * bit) < bit
        turned = list(rows)
        for k in range(CHUNKS):
            if k & bit:
                continue
            near, far = rows[k], rows[k + bit]
            turned[k] = jnp.where(clear, near, pltpu.roll(far, PER * bit, 1))
            turned[k + bit] = jnp.where(clear, pltpu.roll(near, 128 - PER * bit, 1), far)
        rows = turned
    for j in range(4):
        even, uneven = rows[2 * j], rows[2 * j + 1]
        gres_v[:, 128 * j : 128 * j + 128] = jnp.where(
            lane < 64, even, pltpu.roll(uneven, 64, 1)
        )
        grate_v[:, 128 * j : 128 * j + 128] = jnp.where(
            lane < 64, pltpu.roll(even, 64, 1), uneven
        )
    out[4].start()
    out[5].start()

    for copy in out:
        copy.wait()


def per_device(query_rows, key_rows, value_rows, grad_rows, residues, decay_rates):
    rows, width = query_rows.shape
    any_spec = pl.BlockSpec(memory_space=pl.ANY)
    vmem_spec = pl.BlockSpec(memory_space=pltpu.VMEM)
    vmem_limit = 16 * 1024 * 1024
    wide = jax.ShapeDtypeStruct((rows, width), BF16)
    small = jax.ShapeDtypeStruct((MODES, 512), F32)
    dma = pltpu.SemaphoreType.DMA
    whole = pltpu.VMEM((rows, width), BF16)
    outs = pl.pallas_call(
        kernel,
        out_shape=(whole, whole, whole, whole, pltpu.VMEM((CHUNKS, MODES, 128), BF16)),
        in_specs=[any_spec] * 6,
        out_specs=[vmem_spec] * 5,
        scratch_shapes=[whole] * 4
        + [
            pltpu.VMEM((2, MODES, 128), F32),
            pltpu.VMEM((64, 32, 128), BF16),
            pltpu.VMEM((CHUNKS, PER, 128), F32),
            pltpu.VMEM((CHUNKS, TOK, 128), BF16),
            pltpu.VMEM((CHUNKS, TOK, 256), BF16),
            pltpu.VMEM((CHUNKS, TOK, 256), F32),
            pltpu.VMEM((CHUNKS, PER, 128), F32),
            pltpu.VMEM((CHUNKS, 64, 128), BF16),
            pltpu.VMEM((PLANE, 64, 128), BF16),
            pltpu.VMEM((MODES, 128), BF16),
            pltpu.VMEM((PLANE, MODES, 128), BF16),
            pltpu.VMEM((32, 128), F32),
            pltpu.VMEM((32, 128), F32),
            pltpu.VMEM((MODES, 128), F32),
            pltpu.VMEM((MODES, 128), F32),
            pltpu.VMEM((MODES, 128), F32),
            pltpu.VMEM((PLANE, 32, 128), BF16),
            pltpu.VMEM((CHUNKS, 32, 128), BF16),
            pltpu.VMEM((MODES, 128), BF16),
            pltpu.VMEM((16, MODES, 128), BF16),
            pltpu.VMEM((MODES, 128), BF16),
            dma((4,)),
            dma((2,)),
            dma((6,)),
        ]
        + [dma(())] * 7
        + [pltpu.SemaphoreType.REGULAR],
        compiler_params=pltpu.CompilerParams(
            collective_id=0, has_side_effects=True, vmem_limit_bytes=vmem_limit
        ),
    )(
        *(
            pltpu.with_memory_space_constraint(x, pltpu.HBM)
            for x in (query_rows, key_rows, value_rows, grad_rows, residues.T, decay_rates.T)
        )
    )
    op, gq, gk, gv, gres, grate = pl.pallas_call(
        hand_over,
        out_shape=(wide, wide, wide, wide, small, small),
        in_specs=[vmem_spec] * 5,
        out_specs=[any_spec] * 6,
        scratch_shapes=[pltpu.VMEM((MODES, 512), F32)] * 2 + [dma((6,))],
        compiler_params=pltpu.CompilerParams(vmem_limit_bytes=vmem_limit),
    )(*outs)
    return op, gq, gk, gv, gres.T, grate.T


def solution(mesh):
    wide = P("ctx", "tensor")
    return jax.shard_map(
        per_device,
        mesh=mesh,
        in_specs=(wide, wide, wide, wide, P(), P()),
        out_specs=(wide, wide, wide, wide, P(), P()),
        check_vma=False,
    )
```
